32 devices in a mesh: clip: 4 (over z), cam: 2 (over y), slab: 4 (over x, core).
Axes of the slice: x: 2, y: 2, z: 4, core: 2. Of those that a mesh axis runs over, the one named last changes fastest.
Arguments:
- t_query: bfloat16 [8, 512, 1408], P(('clip', 'cam'), 'slab'), parts along dimension 0, may hold values from -8 to 8
- t_key: bfloat16 [8, 512, 1408], P(('clip', 'cam'), 'slab'), parts along dimension 0, may hold values from -6 to 6
- t_value: bfloat16 [8, 512, 1408], P(('clip', 'cam'), 'slab'), parts along dimension 0, may hold values from -6 to 6
- t_resid: bfloat16 [8, 512, 1408], P(('clip', 'cam'), 'slab'), parts along dimension 0, may hold values from -8 to 8
- w_out_teacher: bfloat16 [1408, 1408], P(('cam', 'slab')), may hold values from -0.15625 to 0.15625
- pred_query: bfloat16 [8, 384, 384], P(('clip', 'cam'), 'slab'), parts along dimension 0, may hold values from -6 to 6
- pred_context: bfloat16 [8, 128, 384], P(('clip', 'cam'), 'slab'), parts along dimension 0, may hold values from -6 to 6
- w_query: bfloat16 [384, 384], P(('cam', 'slab')), may hold values from -1 to 1
- w_key: bfloat16 [384, 384], P(('cam', 'slab')), may hold values from -1 to 1
- w_value: bfloat16 [384, 384], P(('cam', 'slab')), may hold values from -0.3125 to 0.3125
- w_out: bfloat16 [384, 384], P(('cam', 'slab')), may hold values from -0.3125 to 0.3125
- w_proj: bfloat16 [384, 1408], P(('cam', 'slab')), may hold values from -0.3125 to 0.3125
- mask_list: int32 [8, 384], P(('clip', 'cam'), 'slab'), parts along dimension 0, may hold values from 0 to 127, as said below
- owners: int32 [8, 384], P('clip'), parts along dimension 0, may hold values from 0 to 7, as said below
Outputs:
- errors: bfloat16 [8, 4, 192, 1408], P(('clip', 'cam'), 'slab'), parts along dimension 0
The draws below stay inside these ranges and needn't reach their ends.
There are 4 independent parts, one for each index of `clip`. The reference program is written for one: setup_inputs(seed, part) draws one part's arguments, and reference() takes and returns one part's arrays. A program takes and returns all parts, laid end to end along the dimension named above; an argument that names none is the same for every part. Nothing has to cross between parts.
Inputs may be any that keep to these rules, and one draw needn't show every extreme that they name: `mask_list`: each camera slab lists 96 distinct local token indices in increasing order. `owners`: an owner is the device cam * 4 + slab of the same clip. Each camera slab names each owner at most 24 times, and in every draw one owner is named exactly 24 times by every camera slab.
All inputs are finite; a program needn't handle non-finite values.
Results may differ from the reference program's by a relative error of at most 0.0076.
Values may be sent and summed in bfloat16 or wider, within the bound.
No kernel may reach another device: no remote copies, remote signals or barrier semaphores. Data moves between devices by JAX's collectives and lax.ppermute only.
A program may use at most 64 MiB of HBM per device.

```python
import math
import jax
import jax.numpy as jnp
from jax import lax

D = 1408
HEADS = 16
P_D = 384
P_HEADS = 12
TOK_DEV = 128
SEQ = 512
M_DEV = 96
CTX_DEV = 32
CAP = 24
N_CAM = 2
N_SLAB = 4


def masked_rows(key):
    subkeys = jax.random.split(jax.random.fold_in(key, 101), N_CAM * N_SLAB)

    def per_device(device_key):
        shuffled = jax.random.permutation(device_key, TOK_DEV)
        return jnp.sort(shuffled[:M_DEV])
    return jax.vmap(per_device)(subkeys).astype(jnp.int32).reshape(N_CAM, N_SLAB, M_DEV)


def draw_mask_list(key, part):
    return masked_rows(key).reshape(N_CAM, N_SLAB * M_DEV)


def draw_owners(key, part):
    devices = N_CAM * N_SLAB
    slot_count = devices * CAP
    busy_owner = jax.random.randint(jax.random.fold_in(key, 202), (), 0, devices)
    subkeys = jax.random.split(jax.random.fold_in(key, 203), devices)
    dest_of_slot = jnp.arange(slot_count, dtype=jnp.int32) // CAP

    def per_device(device_key):
        first_key, second_key = jax.random.split(device_key)
        shuffled = jax.random.permutation(first_key, slot_count).astype(jnp.int32)
        priority = jnp.where(dest_of_slot == busy_owner, -1 - jnp.arange(slot_count, dtype=jnp.int32), shuffled)
        picked = jnp.argsort(priority)[:M_DEV]
        return jax.random.permutation(second_key, dest_of_slot[picked])
    return jax.vmap(per_device)(subkeys).astype(jnp.int32).reshape(N_CAM, N_SLAB * M_DEV)


def draw_t_query(key, part):
    shape = (N_CAM, N_SLAB * TOK_DEV, D)
    base = 2.0 * jax.random.truncated_normal(jax.random.fold_in(key, 11), -4.0, 4.0, shape)
    return base.astype(jnp.bfloat16)


def draw_t_key(key, part):
    shape = (N_CAM, N_SLAB * TOK_DEV, D)
    base = jax.random.truncated_normal(jax.random.fold_in(key, 12), -6.0, 6.0, shape)
    return base.astype(jnp.bfloat16)


def draw_t_resid(key, part):
    shape = (N_CAM, N_SLAB * TOK_DEV, D)
    base = 0.5 * jax.random.truncated_normal(jax.random.fold_in(key, 14), -6.0, 6.0, shape)
    return base.astype(jnp.bfloat16)


def draw_pred_context(key, part):
    shape = (N_CAM, N_SLAB * CTX_DEV, P_D)
    base = jax.random.truncated_normal(jax.random.fold_in(key, 21), -6.0, 6.0, shape)
    return base.astype(jnp.bfloat16)


def draw_pred_query(key, part):
    shape = (N_CAM, N_SLAB * M_DEV, P_D)
    base = jax.random.truncated_normal(jax.random.fold_in(key, 23), -6.0, 6.0, shape)
    return base.astype(jnp.bfloat16)


def draw_w_query(key, part):
    return (jax.random.truncated_normal(jax.random.fold_in(key, 401), -4.0, 4.0, (P_D, P_D)) * (2.0 / math.sqrt(P_D))).astype(jnp.bfloat16)


def draw_w_key(key, part):
    return (jax.random.truncated_normal(jax.random.fold_in(key, 404), -4.0, 4.0, (P_D, P_D)) * (1.0 / math.sqrt(P_D))).astype(jnp.bfloat16)


def steps_of(own_key, shape, cuts, low, high):
    def one(dim, blocks):
        heights = jax.random.uniform(jax.random.fold_in(jax.random.fold_in(own_key, 6), dim), (blocks,), jnp.float32, low / len(cuts), high / len(cuts))
        return jnp.repeat(jnp.exp(heights), shape[dim] // blocks).reshape((-1,) + (1,) * (len(shape) - dim - 1))

    loudness = one(*cuts[0])
    for cut in cuts[1:]:
        loudness = loudness * one(*cut)
    return loudness


def bell_draw(rng, dims, spread, reach, cuts=(), kind=jnp.bfloat16):
    factor_of = steps_of(rng, dims, cuts, -0.22, 0.18) if cuts else 1.0
    drawn = jax.random.normal(rng, dims, jnp.float32) * spread * factor_of
    return jnp.minimum(jnp.maximum(drawn, -reach), reach).astype(kind)


def setup_inputs(seed: int = 0, part: int = 0) -> dict:
    splits = jax.random.split(jax.random.key(seed), 15)
    part_keys = jax.random.split(jax.random.fold_in(splits[14], part), 15)
    return {
        "t_query": draw_t_query(jax.random.fold_in(jax.random.fold_in(splits[14], part), 71), part),
        "t_key": draw_t_key(jax.random.fold_in(jax.random.fold_in(splits[14], part), 71), part),
        "t_value": bell_draw(part_keys[2], (N_CAM, SEQ, D), 1.0, 6.0, ((0, 2), (1, 4))),
        "t_resid": draw_t_resid(jax.random.fold_in(jax.random.fold_in(splits[14], part), 71), part),
        "w_out_teacher": bell_draw(splits[4], (D, D), D ** -0.5, 0.15625, ((0, 8),)),
        "pred_query": draw_pred_query(jax.random.fold_in(jax.random.fold_in(splits[14], part), 71), part),
        "pred_context": draw_pred_context(jax.random.fold_in(jax.random.fold_in(splits[14], part), 71), part),
        "w_query": draw_w_query(jax.random.fold_in(splits[14], 71), part),
        "w_key": draw_w_key(jax.random.fold_in(splits[14], 71), part),
        "w_value": bell_draw(splits[9], (P_D, P_D), P_D ** -0.5, 0.3125, ((0, 8),)),
        "w_out": bell_draw(splits[10], (P_D, P_D), P_D ** -0.5, 0.3125, ((0, 8),)),
        "w_proj": bell_draw(splits[11], (P_D, D), P_D ** -0.5, 0.3125, ((0, 8),)),
        "mask_list": draw_mask_list(jax.random.fold_in(jax.random.fold_in(splits[14], part), 71), part),
        "owners": draw_owners(jax.random.fold_in(jax.random.fold_in(splits[14], part), 71), part),
    }


def norm_rows(values_in):
    average = lax.optimization_barrier(jnp.mean(values_in, axis=-1, keepdims=True))
    centered = values_in - average
    variance = lax.optimization_barrier(jnp.mean(centered * centered, axis=-1, keepdims=True))
    return centered * lax.rsqrt(variance + 1e-06)

def attend(query_rows, key_rows, value_rows, head_count):
    row_count = query_rows.shape[0]
    head_size = query_rows.shape[1] // head_count
    queries = query_rows.reshape(row_count, head_count, head_size).astype(jnp.float32)
    keys_float = key_rows.reshape(-1, head_count, head_size).astype(jnp.float32)
    values_float = value_rows.reshape(-1, head_count, head_size).astype(jnp.float32)
    scores = jnp.einsum('rhd,khd->rhk', queries, keys_float) / math.sqrt(head_size)
    row_max = lax.optimization_barrier(jnp.max(scores, axis=2, keepdims=True))
    exponent = jnp.exp(scores - row_max)
    row_sum = lax.optimization_barrier(jnp.sum(exponent, axis=2))
    rounded = lax.optimization_barrier(exponent.astype(jnp.bfloat16))
    mixed = jnp.einsum('rhk,khd->rhd', rounded.astype(jnp.float32), values_float)
    mixed = mixed / row_sum[:, :, None]
    return mixed.reshape(row_count, head_count * head_size).astype(jnp.bfloat16)

def reference(t_query, t_key, t_value, t_resid, w_out_teacher, pred_query, pred_context, w_query, w_key, w_value, w_out, w_proj, mask_list, owners):

    def teacher_camera(camera_inputs):
        query_cam, key_cam, value_cam, resid_cam = camera_inputs
        attended = attend(query_cam, key_cam, value_cam, HEADS)
        summed = resid_cam.astype(jnp.float32) + jnp.dot(attended, w_out_teacher, preferred_element_type=jnp.float32)
        return norm_rows(summed).astype(jnp.bfloat16)
    targets = lax.map(teacher_camera, (t_query, t_key, t_value, t_resid))
    devices = N_CAM * N_SLAB
    slot_count = devices * CAP
    masked_lists = mask_list.reshape(devices, M_DEV).astype(jnp.int32)
    owner_lists = owners.reshape(devices, M_DEV).astype(jnp.int32)
    device_rows = targets.reshape(devices, TOK_DEV, D)
    picked = jnp.take_along_axis(device_rows, masked_lists[:, :, None], axis=1)
    onehot = (owner_lists[:, :, None] == jnp.arange(devices, dtype=jnp.int32)[None, None, :]).astype(jnp.int32)
    earlier = jnp.cumsum(onehot, axis=1) - onehot
    slot_rank = lax.optimization_barrier(jnp.sum(onehot * earlier, axis=2)).astype(jnp.int32)
    flat_slot = owner_lists * slot_count + jnp.arange(devices, dtype=jnp.int32)[:, None] * CAP + slot_rank
    flat_slot = flat_slot.reshape(-1)
    target_slots = jnp.zeros((devices * slot_count, D), jnp.bfloat16).at[flat_slot].set(picked.reshape(-1, D))
    query_slots = jnp.zeros((devices * slot_count, P_D), jnp.bfloat16).at[flat_slot].set(pred_query.reshape(-1, P_D))
    occupied = jnp.zeros((devices * slot_count,), jnp.bool_).at[flat_slot].set(True)
    context_all = pred_context.reshape(-1, P_D)
    context_keys = jnp.dot(context_all, w_key, preferred_element_type=jnp.float32).astype(jnp.bfloat16)
    context_values = jnp.dot(context_all, w_value, preferred_element_type=jnp.float32).astype(jnp.bfloat16)
    pred_q = jnp.dot(query_slots, w_query, preferred_element_type=jnp.float32).astype(jnp.bfloat16)

    def owner_rows(owner_inputs):
        q_owner, input_owner, target_owner, filled_owner = owner_inputs
        attended = attend(q_owner, context_keys, context_values, P_HEADS)
        hidden = input_owner.astype(jnp.float32) + jnp.dot(attended, w_out, preferred_element_type=jnp.float32)
        predicted = norm_rows(hidden).astype(jnp.bfloat16)
        difference = jnp.dot(predicted, w_proj, preferred_element_type=jnp.float32) - target_owner.astype(jnp.float32)
        return jnp.where(filled_owner[:, None], difference, 0.0).astype(jnp.bfloat16)
    errors = lax.map(owner_rows, (pred_q.reshape(devices, slot_count, P_D), query_slots.reshape(devices, slot_count, P_D), target_slots.reshape(devices, slot_count, D), occupied.reshape(devices, slot_count)))
    return errors.reshape(N_CAM, N_SLAB, slot_count, D)
```

```python
import math

import jax
import jax.numpy as jnp
from jax import lax
from jax.sharding import PartitionSpec as P

HEADS = 16
P_HEADS = 12


def norm_rows(values_in):
    average = jnp.mean(values_in, axis=-1, keepdims=True)
    centered = values_in - average
    variance = jnp.mean(centered * centered, axis=-1, keepdims=True)
    return centered * lax.rsqrt(variance + 1e-06)


def empty_state(row_count, head_count, head_size):
    return (
        jnp.full((row_count, head_count), -1e30, jnp.float32),
        jnp.zeros((row_count, head_count), jnp.float32),
        jnp.zeros((row_count, head_count, head_size), jnp.float32),
    )


def attend_block(state_now, query_heads, key_rows, value_rows):
    head_count = query_heads.shape[1]
    head_size = query_heads.shape[2]
    running_max, weight_sum, accumulated = state_now
    for offset in range(0, key_rows.shape[0], 512):
        key_block = key_rows[offset : offset + 512].reshape(-1, head_count, head_size)
        value_block = value_rows[offset : offset + 512].reshape(-1, head_count, head_size)
        scores = jnp.einsum(
            "rhd,khd->rhk", query_heads, key_block, preferred_element_type=jnp.float32
        ) / math.sqrt(head_size)
        new_max = jnp.maximum(running_max, jnp.max(scores, axis=2))
        rescale = jnp.exp(running_max - new_max)
        exponent = jnp.exp(scores - new_max[:, :, None])
        weight_sum = weight_sum * rescale + jnp.sum(exponent, axis=2)
        accumulated = accumulated * rescale[:, :, None] + jnp.einsum(
            "rhk,khd->rhd",
            exponent.astype(jnp.bfloat16),
            value_block,
            preferred_element_type=jnp.float32,
        )
        running_max = new_max
    return (running_max, weight_sum, accumulated)


def finish_heads(weight_sum, accumulated):
    mixed = accumulated / weight_sum[:, :, None]
    return mixed.reshape(mixed.shape[0], -1).astype(jnp.bfloat16)


def shards(
    t_query,
    t_key,
    t_value,
    t_resid,
    w_out_teacher,
    pred_query,
    pred_context,
    w_query,
    w_key,
    w_value,
    w_out,
    w_proj,
    mask_list,
    owners,
):
    model_width = t_query.shape[2]
    head_size = model_width // HEADS
    local_rows = mask_list[0]
    masked_count = local_rows.shape[0]
    masked_query = jnp.take(t_query[0], local_rows, axis=0)
    masked_resid = jnp.take(t_resid[0], local_rows, axis=0)
    query_heads = masked_query.reshape(masked_count, HEADS, head_size)
    pieces = (
        lax.all_gather(t_key[0], "slab", axis=0, tiled=True),
        lax.all_gather(t_value[0], "slab", axis=0, tiled=True),
    )
    running_max, weight_sum, accumulated = attend_block(
        empty_state(masked_count, HEADS, head_size), query_heads, pieces[0], pieces[1]
    )
    teacher_attended = finish_heads(weight_sum, accumulated)
    projected = jnp.dot(
        teacher_attended,
        lax.all_gather(w_out_teacher, ("cam", "slab"), axis=0, tiled=True),
        preferred_element_type=jnp.float32,
    )
    targets = norm_rows(masked_resid.astype(jnp.float32) + projected).astype(jnp.bfloat16)
    devices = lax.axis_size(("cam", "slab"))
    capacity = 2 * masked_count // devices
    myself = lax.axis_index(("cam", "slab"))
    own_dest = lax.dynamic_index_in_dim(
        owners.reshape(devices, masked_count), myself, 0, keepdims=False
    )
    earlier = jnp.tril(jnp.ones((masked_count, masked_count), jnp.bool_), -1)
    same_owner = own_dest[:, None] == own_dest[None, :]
    order_rank = jnp.sum((same_owner & earlier).astype(jnp.int32), axis=1)
    slot_index = own_dest * capacity + order_rank
    slot_total = devices * capacity
    query_rows = pred_query[0]
    pred_width = query_rows.shape[1]
    full_query, full_key, full_value, full_out, full_proj = (
        lax.all_gather(w_query, ("cam", "slab"), axis=0, tiled=True),
        lax.all_gather(w_key, ("cam", "slab"), axis=0, tiled=True),
        lax.all_gather(w_value, ("cam", "slab"), axis=0, tiled=True),
        lax.all_gather(w_out, ("cam", "slab"), axis=0, tiled=True),
        lax.all_gather(w_proj, ("cam", "slab"), axis=0, tiled=True),
    )
    pred_head = pred_width // P_HEADS
    pred_heads = (
        jnp.dot(query_rows, full_query, preferred_element_type=jnp.float32)
        .astype(jnp.bfloat16)
        .reshape(masked_count, P_HEADS, pred_head)
    )
    start_state = empty_state(masked_count, P_HEADS, pred_head)
    context = lax.all_gather(pred_context[0], ("cam", "slab"), axis=0, tiled=True)
    context_keys = jnp.dot(context, full_key, preferred_element_type=jnp.float32)
    context_values = jnp.dot(context, full_value, preferred_element_type=jnp.float32)
    running_max, weight_sum, accumulated = attend_block(
        start_state,
        pred_heads,
        context_keys.astype(jnp.bfloat16),
        context_values.astype(jnp.bfloat16),
    )
    pred_attended = finish_heads(weight_sum, accumulated)
    pred_hidden = query_rows.astype(jnp.float32) + jnp.dot(
        pred_attended, full_out, preferred_element_type=jnp.float32
    )
    predicted = norm_rows(pred_hidden).astype(jnp.bfloat16)
    difference = jnp.dot(
        predicted, full_proj, preferred_element_type=jnp.float32
    ) - targets.astype(jnp.float32)
    sent = (
        jnp.zeros((slot_total, model_width), jnp.bfloat16)
        .at[slot_index]
        .set(difference.astype(jnp.bfloat16))
        .reshape(devices, capacity, model_width)
    )
    errors = lax.all_to_all(sent, ("cam", "slab"), split_axis=0, concat_axis=0, tiled=True)
    return errors.reshape(1, 1, slot_total, model_width)


def solution(mesh):
    placed = (
        P(("clip", "cam"), "slab", None),
        P(("clip", "cam"), "slab", None),
        P(("clip", "cam"), "slab", None),
        P(("clip", "cam"), "slab", None),
        P(("cam", "slab"), None),
        P(("clip", "cam"), "slab", None),
        P(("clip", "cam"), "slab", None),
        P(("cam", "slab"), None),
        P(("cam", "slab"), None),
        P(("cam", "slab"), None),
        P(("cam", "slab"), None),
        P(("cam", "slab"), None),
        P(("clip", "cam"), "slab"),
        P("clip", None),
    )
    return jax.shard_map(
        shards,
        mesh=mesh,
        in_specs=placed,
        out_specs=P(("clip", "cam"), "slab", None, None),
        check_vma=False,
    )
```

```python
import functools
import math

import jax
import jax.numpy as jnp
from jax import lax
from jax.experimental import pallas as pl
from jax.experimental.pallas import tpu as pltpu
from jax.sharding import PartitionSpec as P

HEADS = 16
P_HEADS = 12
LANES = 128


def norm_rows(values_in):
    average = jnp.mean(values_in, axis=-1, keepdims=True)
    centered = values_in - average
    variance = jnp.mean(centered * centered, axis=-1, keepdims=True)
    return centered * lax.rsqrt(variance + 1e-06)


def empty_state(row_count, head_count, head_size):
    return (
        jnp.full((row_count, head_count), -1e30, jnp.float32),
        jnp.zeros((row_count, head_count), jnp.float32),
        jnp.zeros((row_count, head_count, head_size), jnp.float32),
    )


def attend_block(state_now, query_heads, key_rows, value_rows):
    head_count = query_heads.shape[1]
    head_size = query_heads.shape[2]
    running_max, weight_sum, accumulated = state_now
    for offset in range(0, key_rows.shape[0], 512):
        key_block = key_rows[offset : offset + 512].reshape(-1, head_count, head_size)
        value_block = value_rows[offset : offset + 512].reshape(-1, head_count, head_size)
        scores = jnp.einsum(
            "rhd,khd->rhk", query_heads, key_block, preferred_element_type=jnp.float32
        ) / math.sqrt(head_size)
        new_max = jnp.maximum(running_max, jnp.max(scores, axis=2))
        rescale = jnp.exp(running_max - new_max)
        exponent = jnp.exp(scores - new_max[:, :, None])
        weight_sum = weight_sum * rescale + jnp.sum(exponent, axis=2)
        accumulated = accumulated * rescale[:, :, None] + jnp.einsum(
            "rhk,khd->rhd",
            exponent.astype(jnp.bfloat16),
            value_block,
            preferred_element_type=jnp.float32,
        )
        running_max = new_max
    return (running_max, weight_sum, accumulated)


def finish_heads(weight_sum, accumulated):
    mixed = accumulated / weight_sum[:, :, None]
    return mixed.reshape(mixed.shape[0], -1).astype(jnp.bfloat16)


def shards(
    t_query,
    t_key,
    t_value,
    t_resid,
    w_out_teacher,
    pred_query,
    pred_context,
    w_query,
    w_key,
    w_value,
    w_out,
    w_proj,
    mask_list,
    owners,
):
    model_width = t_query.shape[2]
    head_size = model_width // HEADS
    local_rows = mask_list[0]
    masked_count = local_rows.shape[0]
    masked_query = jnp.take(t_query[0], local_rows, axis=0)
    masked_resid = jnp.take(t_resid[0], local_rows, axis=0)
    query_heads = masked_query.reshape(masked_count, HEADS, head_size)
    pieces = (
        lax.all_gather(t_key[0], "slab", axis=0, tiled=True),
        lax.all_gather(t_value[0], "slab", axis=0, tiled=True),
    )
    running_max, weight_sum, accumulated = attend_block(
        empty_state(masked_count, HEADS, head_size), query_heads, pieces[0], pieces[1]
    )
    teacher_attended = finish_heads(weight_sum, accumulated)
    projected = jnp.dot(
        teacher_attended,
        lax.all_gather(w_out_teacher, ("cam", "slab"), axis=0, tiled=True),
        preferred_element_type=jnp.float32,
    )
    targets = norm_rows(masked_resid.astype(jnp.float32) + projected).astype(jnp.bfloat16)
    devices = lax.axis_size(("cam", "slab"))
    capacity = 2 * masked_count // devices
    myself = lax.axis_index(("cam", "slab"))
    own_dest = lax.dynamic_index_in_dim(
        owners.reshape(devices, masked_count), myself, 0, keepdims=False
    )
    earlier = jnp.tril(jnp.ones((masked_count, masked_count), jnp.bool_), -1)
    same_owner = own_dest[:, None] == own_dest[None, :]
    order_rank = jnp.sum((same_owner & earlier).astype(jnp.int32), axis=1)
    slot_index = own_dest * capacity + order_rank
    slot_total = devices * capacity
    query_rows = pred_query[0]
    pred_width = query_rows.shape[1]
    full_query, full_key, full_value, full_out, full_proj = (
        lax.all_gather(w_query, ("cam", "slab"), axis=0, tiled=True),
        lax.all_gather(w_key, ("cam", "slab"), axis=0, tiled=True),
        lax.all_gather(w_value, ("cam", "slab"), axis=0, tiled=True),
        lax.all_gather(w_out, ("cam", "slab"), axis=0, tiled=True),
        lax.all_gather(w_proj, ("cam", "slab"), axis=0, tiled=True),
    )
    pred_head = pred_width // P_HEADS
    pred_heads = (
        jnp.dot(query_rows, full_query, preferred_element_type=jnp.float32)
        .astype(jnp.bfloat16)
        .reshape(masked_count, P_HEADS, pred_head)
    )
    start_state = empty_state(masked_count, P_HEADS, pred_head)
    context = lax.all_gather(pred_context[0], ("cam", "slab"), axis=0, tiled=True)
    context_keys = jnp.dot(context, full_key, preferred_element_type=jnp.float32)
    context_values = jnp.dot(context, full_value, preferred_element_type=jnp.float32)
    running_max, weight_sum, accumulated = attend_block(
        start_state,
        pred_heads,
        context_keys.astype(jnp.bfloat16),
        context_values.astype(jnp.bfloat16),
    )
    pred_attended = finish_heads(weight_sum, accumulated)
    pred_hidden = query_rows.astype(jnp.float32) + jnp.dot(
        pred_attended, full_out, preferred_element_type=jnp.float32
    )
    predicted = norm_rows(pred_hidden).astype(jnp.bfloat16)
    difference = jnp.dot(
        predicted, full_proj, preferred_element_type=jnp.float32
    ) - targets.astype(jnp.float32)
    sent = (
        jnp.zeros((slot_total, model_width), jnp.bfloat16)
        .at[slot_index]
        .set(difference.astype(jnp.bfloat16))
        .reshape(devices, capacity, model_width)
    )
    errors = lax.all_to_all(sent, ("cam", "slab"), split_axis=0, concat_axis=0, tiled=True)
    return errors.reshape(1, 1, slot_total, model_width)


def rows_dot(left, right):
    return lax.dot_general(
        left, right, (((1,), (1,)), ((), ())), preferred_element_type=jnp.float32
    )


def dot(left, right):
    return jnp.dot(left, right, preferred_element_type=jnp.float32)


def position():
    return lax.axis_index("cam"), lax.axis_index("slab")


def head_windows(head_count, head_size):
    windows = []
    for head in range(head_count):
        low, high = head * head_size, (head + 1) * head_size
        start = low // LANES * LANES
        windows.append((low, high, start, -(-high // LANES) * LANES))
    return windows


def inside(shape, start, low, high):
    lane = lax.broadcasted_iota(jnp.int32, shape, 1) + start
    return (lane >= low) & (lane < high)


def softmax_terms(scores, scale):
    peak = jnp.max(scores, axis=1, keepdims=True)
    terms = jnp.exp2((scores - peak) * scale)
    return terms.astype(jnp.bfloat16), jnp.sum(terms, axis=1, keepdims=True)


def slot_picker(key_row, owner, capacity, slot_total):
    shape = (2 * capacity, key_row.shape[1])
    row = lax.broadcasted_iota(jnp.int32, shape, 0)
    late = row >= capacity
    wanted = owner * capacity + row + jnp.where(late, slot_total - capacity, 0)
    return jnp.where(key_row == wanted, 1.0, 0.0).astype(jnp.bfloat16)


def pack_kernel(
    capacity, query, key, value, resid, mask, owners, wq, wk, wv, wo, wp, context,
    block0, block1, block2, block3, resid_rows, slot_keys, pack, stack, blocks,
):
    cam, slab = position()
    tokens, width = key.shape
    masked = mask.shape[1]
    quarter = width // 8
    token = lax.broadcasted_iota(jnp.int32, (tokens, masked), 0)
    chosen = jnp.where(token == mask[...], 1.0, 0.0).T.astype(jnp.bfloat16)
    stack[0:tokens] = key[...]
    stack[tokens : 2 * tokens] = value[...]
    stack[2 * tokens :] = dot(chosen, query[...]).astype(jnp.bfloat16)
    resid_rows[...] = dot(chosen, resid[...]).astype(jnp.bfloat16)
    row_total = stack.shape[0]
    pad = blocks.shape[2] - 2 * quarter
    for other in range(4):
        first = stack[:, other * quarter : (other + 1) * quarter]
        second = stack[:, (other + 4) * quarter : (other + 5) * quarter]
        blocks[other] = jnp.concatenate(
            [first, second, jnp.zeros((row_total, pad), jnp.bfloat16)], axis=1
        )
    for relation, out in enumerate((block0, block1, block2, block3)):
        out[...] = blocks[slab ^ relation]
    listed = owners.shape[1]
    before = lax.broadcasted_iota(jnp.int32, (listed, listed), 0)
    after = lax.broadcasted_iota(jnp.int32, (listed, listed), 1)
    group = sum((before >= edge).astype(jnp.int32) for edge in range(masked, listed, masked))
    group_after = sum((after >= edge).astype(jnp.int32) for edge in range(masked, listed, masked))
    precedes = jnp.where((before < after) & (group == group_after), 1.0, 0.0)
    owner_row = owners[pl.ds(cam, 1), :]
    device = lax.broadcasted_iota(jnp.int32, (8, listed), 0)
    owned = jnp.where(device == owner_row, 1.0, 0.0)
    counted = dot(owned.astype(jnp.bfloat16), precedes.astype(jnp.bfloat16))
    rank = jnp.sum(owned * counted, axis=0, keepdims=True).astype(jnp.int32)
    lane = lax.broadcasted_iota(jnp.int32, (1, listed), 1)
    odd = ((lane >= masked) & (lane < 2 * masked)) | (lane >= 3 * masked)
    keys = owner_row * capacity + rank + jnp.where(odd, 8 * capacity, 0)
    slot_keys[0:1, :] = keys[:, 0 : 2 * masked]
    slot_keys[1:2, :] = keys[:, 2 * masked :]
    at = 0
    for part in (wq, wk, wv, wo, wp):
        pack[:, at : at + part.shape[1]] = part[...]
        at += part.shape[1]
    pack[0 : context.shape[0], at:] = context[...]
    pack[context.shape[0] :, at:] = jnp.zeros(
        (pack.shape[0] - context.shape[0], context.shape[1]), jnp.bfloat16
    )


def ask_kernel(capacity, slot_keys, own_rows, peer_rows, pack, out0, out1, out2, out3, pair):
    cam, slab = position()
    rows = own_rows.shape[0]
    core = slab % 2
    pair[pl.ds(pl.multiple_of(core * rows, rows), rows)] = own_rows[...]
    pair[pl.ds(pl.multiple_of((1 - core) * rows, rows), rows)] = peer_rows[...]
    key_row = slot_keys[pl.ds(slab // 2, 1), :]
    width = pack.shape[1]
    for relation, out in enumerate((out0, out1, out2, out3)):
        owner = (cam * 4 + slab) ^ (relation * 2)
        picker = slot_picker(key_row, owner, capacity, 8 * capacity)
        picked = dot(picker, pair[...]).astype(jnp.bfloat16)
        if relation:
            out[:, 0:width] = pack[...]
            out[:, width:] = picked
        else:
            out[...] = picked


def teacher_kernel(
    capacity, head_size, tokens, masked, slot_keys, block0, block1, block2, block3,
    own_core, peer_core, queries, keys, values, attended,
):
    cam, slab = position()
    for relation, block in enumerate((block0, block1, block2, block3)):
        other = slab ^ relation
        keys[relation * tokens : (relation + 1) * tokens] = block[0:tokens]
        values[relation * tokens : (relation + 1) * tokens] = block[tokens : 2 * tokens]
        queries[pl.ds(pl.multiple_of(other * masked, masked), masked)] = block[2 * tokens :]
    scale = math.log2(math.e) / math.sqrt(head_size)
    chunk = 2 * masked
    for half in range(2):
        rows = slice(half * chunk, (half + 1) * chunk)
        total = [jnp.zeros((chunk, LANES), jnp.float32) for _ in range(attended.shape[1] // LANES)]
        for low, high, start, stop in head_windows(4, head_size):
            window = inside((chunk, stop - start), start, low, high)
            picked = jnp.where(window, queries[rows, start:stop].astype(jnp.float32), 0.0)
            scores = rows_dot(picked.astype(jnp.bfloat16), keys[:, start:stop])
            terms, weight = softmax_terms(scores, scale)
            mixed = dot(terms, values[:, start:stop]) / weight
            mixed = jnp.where(window, mixed, 0.0)
            for tile in range(start // LANES, stop // LANES):
                total[tile] += mixed[:, tile * LANES - start : (tile + 1) * LANES - start]
        attended[rows] = jnp.concatenate(total, axis=1).astype(jnp.bfloat16)
    for flip, out in enumerate((own_core, peer_core)):
        for relation in range(4):
            owner = (cam * 4 + slab) ^ (relation * 2 + flip)
            for half in range(2):
                picker = slot_picker(slot_keys[half : half + 1, :], owner, capacity, 8 * capacity)
                at = (relation * 2 + half) * 2 * capacity
                out[at : at + 2 * capacity] = dot(
                    picker, attended[half * chunk : (half + 1) * chunk]
                ).astype(jnp.bfloat16)


def project_kernel(
    capacity, slot_keys, own_slots, peer_slots, w_own, w_cam, w_core, w_both, resid_own, resid_peer,
    out0, out1, out2, out3, weight, resid_pair, total,
):
    cam, slab = position()
    core, chip = slab % 2, slab // 2
    part, width = w_own.shape
    half = own_slots.shape[1]
    for base, same, crossed in ((0, w_own, w_cam), (half, w_core, w_both)):
        weight[pl.ds(pl.multiple_of(base + cam * part, 16), part)] = same[...]
        weight[pl.ds(pl.multiple_of(base + (1 - cam) * part, 16), part)] = crossed[...]
        weight[base + 2 * part : base + half] = jnp.zeros((half - 2 * part, width), jnp.bfloat16)
    rows = resid_own.shape[0]
    resid_pair[pl.ds(pl.multiple_of(core * rows, rows), rows)] = resid_own[...]
    resid_pair[pl.ds(pl.multiple_of((1 - core) * rows, rows), rows)] = resid_peer[...]
    key_row = slot_keys[pl.ds(chip, 1), :]
    block = out0.shape[0]
    for relation, out in ((3, out3), (2, out2), (1, out1), (0, out0)):
        at = relation * block
        total[...] = dot(own_slots[at : at + block], weight[0:half]) + dot(
            peer_slots[at : at + block], weight[half:]
        )
        owner = (cam * 4 + slab) ^ (relation * 2)
        picker = slot_picker(key_row, owner, capacity, 8 * capacity)
        own_rows = pl.ds(pl.multiple_of(chip * 2 * capacity, 8), 2 * capacity)
        total[own_rows] = total[own_rows] + dot(picker, resid_pair[...])
        out[...] = total[...].astype(jnp.bfloat16)


def predict_kernel(
    context_rows, ask0, ask1, ask2, ask3, own_pack, peer0, peer1, peer2, peer3, out,
    queries, weights, context,
):
    cam, slab = position()
    rows, width = ask0.shape
    own = cam * 4 + slab
    side = own // 2
    pieces = ((own_pack, peer0), (ask1, peer1), (ask2, peer2), (ask3, peer3))
    wide = weights.shape[1]
    for relation, both in enumerate(pieces):
        asked = ask0[...] if relation == 0 else both[0][:, wide + width :]
        queries[pl.ds(pl.multiple_of((side ^ relation) * rows, rows), rows)] = asked
        for flip, piece in enumerate(both):
            source = own ^ (relation * 2 + flip)
            part = piece.shape[0]
            weights[pl.ds(pl.multiple_of(source * part, part), part)] = piece[:, 0:wide]
            context[pl.ds(pl.multiple_of(source * context_rows, context_rows), context_rows)] = (
                piece[0:context_rows, wide : wide + width]
            )
    head_size = width // P_HEADS
    scale = math.log2(math.e) / math.sqrt(head_size)
    asked = dot(queries[...], weights[:, 0:width]).astype(jnp.bfloat16)
    seen_keys = dot(context[...], weights[:, width : 2 * width]).astype(jnp.bfloat16)
    seen_values = dot(context[...], weights[:, 2 * width : 3 * width]).astype(jnp.bfloat16)
    total = [jnp.zeros((asked.shape[0], LANES), jnp.float32) for _ in range(width // LANES)]
    for low, high, start, stop in head_windows(P_HEADS, head_size):
        window = inside((asked.shape[0], stop - start), start, low, high)
        picked = jnp.where(window, asked[:, start:stop].astype(jnp.float32), 0.0)
        scores = rows_dot(picked.astype(jnp.bfloat16), seen_keys[:, start:stop])
        terms, weight = softmax_terms(scores, scale)
        mixed = dot(terms, seen_values[:, start:stop]) / weight
        total[start // LANES] += jnp.where(window, mixed, 0.0)
    attended = jnp.concatenate(total, axis=1).astype(jnp.bfloat16)
    hidden = queries[...].astype(jnp.float32) + dot(attended, weights[:, 3 * width : 4 * width])
    predicted = norm_rows(hidden).astype(jnp.bfloat16)
    out[...] = dot(predicted, weights[:, 4 * width :])


def finish_kernel(capacity, masked, owners, predicted, part0, part1, part2, part3, out):
    cam, slab = position()
    rows = part0.shape[0]
    for flip, (near, far) in enumerate(((part0, part1), (part2, part3))):
        camera = cam ^ flip
        at = pl.ds(pl.multiple_of(camera * rows, rows), rows)
        summed = near[...].astype(jnp.float32) + far[...].astype(jnp.float32)
        shape = (rows, owners.shape[1])
        row = lax.broadcasted_iota(jnp.int32, shape, 0)
        lane = lax.broadcasted_iota(jnp.int32, shape, 1)
        listed = owners[pl.ds(camera, 1), :] == cam * 4 + slab
        same = jnp.zeros(shape, jnp.bool_)
        for group in range(4):
            same = same | (
                (row >= group * capacity)
                & (row < (group + 1) * capacity)
                & (lane >= group * masked)
                & (lane < (group + 1) * masked)
            )
        count = jnp.sum(jnp.where(same & listed, 1.0, 0.0), axis=1, keepdims=True)
        order = lax.broadcasted_iota(jnp.int32, (rows, 1), 0)
        order = order - sum(
            jnp.where(order >= group * capacity, capacity, 0) for group in range(1, 4)
        )
        filled = order.astype(jnp.float32) < count
        goal = norm_rows(summed).astype(jnp.bfloat16).astype(jnp.float32)
        out[at] = jnp.where(filled, predicted[at] - goal, 0.0).astype(jnp.bfloat16)


def call(kernel, outs, scratch, *args):
    shapes = tuple(jax.ShapeDtypeStruct(shape, dtype) for shape, dtype in outs)
    return pl.pallas_call(
        kernel,
        out_shape=shapes,
        scratch_shapes=[pltpu.VMEM(shape, dtype) for shape, dtype in scratch],
        compiler_params=pltpu.CompilerParams(vmem_limit_bytes=40 * 2**20),
    )(*args)


def send(rows, flip):
    return lax.ppermute(rows, ("cam", "slab"), [(source, source ^ flip) for source in range(8)])


def paired_shards(
    t_query, t_key, t_value, t_resid, w_out_teacher, pred_query, pred_context,
    w_query, w_key, w_value, w_out, w_proj, mask_list, owners,
):
    bf16, f32 = jnp.bfloat16, jnp.float32
    tokens, width = t_key.shape[1:]
    masked, pred_width = pred_query.shape[1:]
    capacity = masked // 4
    quarter = width // 8
    head_size = width // HEADS
    context_rows = pred_context.shape[1]
    padded = -(-2 * quarter // LANES) * LANES
    block_rows = 2 * tokens + masked
    block = ((block_rows, padded), bf16)
    weight_rows = w_query.shape[0]
    weight_width = 4 * pred_width + w_proj.shape[1]
    pack_width = weight_width + pred_width
    peer_query = send(pred_query[0], 1)
    w_core = send(w_out_teacher, 1)
    w_cam = send(w_out_teacher, 4)
    block0, block1, block2, block3, resid_rows, slot_keys, pack = call(
        functools.partial(pack_kernel, capacity),
        [block] * 4
        + [((masked, width), bf16), ((2, 2 * masked), jnp.int32), ((weight_rows, pack_width), bf16)],
        [((block_rows, width), bf16), ((4, block_rows, padded), bf16)],
        t_query[0], t_key[0], t_value[0], t_resid[0], mask_list, owners,
        w_query, w_key, w_value, w_out, w_proj, pred_context[0],
    )
    other2, other3, other1 = send(block2, 2), send(block3, 3), send(block1, 1)
    w_both = send(w_cam, 1)
    peer_resid = send(resid_rows, 1)
    ask_rows = 2 * capacity
    ask = ((ask_rows, pack_width + pred_width), bf16)
    ask0, ask1, ask2, ask3 = call(
        functools.partial(ask_kernel, capacity),
        [((ask_rows, pred_width), bf16), ask, ask, ask],
        [((2 * masked, pred_width), bf16)],
        slot_keys, pred_query[0], peer_query, pack,
    )
    asked1, asked2, asked3 = send(ask1, 2), send(ask2, 4), send(ask3, 6)
    peer_pack = send(pack, 1)
    slots = ((16 * capacity, padded), bf16)
    own_slots, away_slots = call(
        functools.partial(teacher_kernel, capacity, head_size, tokens, masked),
        [slots, slots],
        [
            ((4 * masked, padded), bf16), ((4 * tokens, padded), bf16), ((4 * tokens, padded), bf16),
            ((4 * masked, padded), bf16),
        ],
        slot_keys, block0, other1, other2, other3,
    )
    peer_slots = send(away_slots, 1)
    part = ((4 * capacity, width), bf16)
    part0, part1, part2, part3 = call(
        functools.partial(project_kernel, capacity),
        [part] * 4,
        [((2 * padded, width), bf16), ((2 * masked, width), bf16), ((4 * capacity, width), f32)],
        slot_keys, own_slots, peer_slots, w_out_teacher, w_cam, w_core, w_both, resid_rows, peer_resid,
    )
    far1, far2, far3 = send(part1, 2), send(part2, 4), send(part3, 6)
    peer1, peer2, peer3 = send(asked1, 1), send(asked2, 1), send(asked3, 1)
    (predicted,) = call(
        functools.partial(predict_kernel, context_rows),
        [((8 * capacity, width), f32)],
        [
            ((8 * capacity, pred_width), bf16), ((8 * weight_rows, weight_width), bf16),
            ((8 * context_rows, pred_width), bf16),
        ],
        ask0, asked1, asked2, asked3, pack, peer_pack, peer1, peer2, peer3,
    )
    (errors,) = call(
        functools.partial(finish_kernel, capacity, masked),
        [((8 * capacity, width), bf16)],
        [],
        owners, predicted, part0, far1, far2, far3,
    )
    return errors[None, None]


def solution(mesh):
    placed = (
        P(("clip", "cam"), "slab", None),
        P(("clip", "cam"), "slab", None),
        P(("clip", "cam"), "slab", None),
        P(("clip", "cam"), "slab", None),
        P(("cam", "slab"), None),
        P(("clip", "cam"), "slab", None),
        P(("clip", "cam"), "slab", None),
        P(("cam", "slab"), None),
        P(("cam", "slab"), None),
        P(("cam", "slab"), None),
        P(("cam", "slab"), None),
        P(("cam", "slab"), None),
        P(("clip", "cam"), "slab"),
        P("clip", None),
    )
    small = (mesh.shape["cam"], mesh.shape["slab"]) == (2, 4)
    return jax.shard_map(
        paired_shards if small else shards,
        mesh=mesh,
        in_specs=placed,
        out_specs=P(("clip", "cam"), "slab", None, None),
        check_vma=False,
    )
```

```python
import functools
import math

import jax
import jax.numpy as jnp
from jax import lax
from jax.experimental import pallas as pl
from jax.experimental.pallas import tpu as pltpu
from jax.sharding import PartitionSpec as P

HEADS = 16
P_HEADS = 12
LANES = 128


def norm_rows(values_in):
    average = jnp.mean(values_in, axis=-1, keepdims=True)
    centered = values_in - average
    variance = jnp.mean(centered * centered, axis=-1, keepdims=True)
    return centered * lax.rsqrt(variance + 1e-06)


def empty_state(row_count, head_count, head_size):
    return (
        jnp.full((row_count, head_count), -1e30, jnp.float32),
        jnp.zeros((row_count, head_count), jnp.float32),
        jnp.zeros((row_count, head_count, head_size), jnp.float32),
    )


def attend_block(state_now, query_heads, key_rows, value_rows):
    head_count = query_heads.shape[1]
    head_size = query_heads.shape[2]
    running_max, weight_sum, accumulated = state_now
    for offset in range(0, key_rows.shape[0], 512):
        key_block = key_rows[offset : offset + 512].reshape(-1, head_count, head_size)
        value_block = value_rows[offset : offset + 512].reshape(-1, head_count, head_size)
        scores = jnp.einsum(
            "rhd,khd->rhk", query_heads, key_block, preferred_element_type=jnp.float32
        ) / math.sqrt(head_size)
        new_max = jnp.maximum(running_max, jnp.max(scores, axis=2))
        rescale = jnp.exp(running_max - new_max)
        exponent = jnp.exp(scores - new_max[:, :, None])
        weight_sum = weight_sum * rescale + jnp.sum(exponent, axis=2)
        accumulated = accumulated * rescale[:, :, None] + jnp.einsum(
            "rhk,khd->rhd",
            exponent.astype(jnp.bfloat16),
            value_block,
            preferred_element_type=jnp.float32,
        )
        running_max = new_max
    return (running_max, weight_sum, accumulated)


def finish_heads(weight_sum, accumulated):
    mixed = accumulated / weight_sum[:, :, None]
    return mixed.reshape(mixed.shape[0], -1).astype(jnp.bfloat16)


def shards(
    t_query,
    t_key,
    t_value,
    t_resid,
    w_out_teacher,
    pred_query,
    pred_context,
    w_query,
    w_key,
    w_value,
    w_out,
    w_proj,
    mask_list,
    owners,
):
    model_width = t_query.shape[2]
    head_size = model_width // HEADS
    local_rows = mask_list[0]
    masked_count = local_rows.shape[0]
    masked_query = jnp.take(t_query[0], local_rows, axis=0)
    masked_resid = jnp.take(t_resid[0], local_rows, axis=0)
    query_heads = masked_query.reshape(masked_count, HEADS, head_size)
    pieces = (
        lax.all_gather(t_key[0], "slab", axis=0, tiled=True),
        lax.all_gather(t_value[0], "slab", axis=0, tiled=True),
    )
    running_max, weight_sum, accumulated = attend_block(
        empty_state(masked_count, HEADS, head_size), query_heads, pieces[0], pieces[1]
    )
    teacher_attended = finish_heads(weight_sum, accumulated)
    projected = jnp.dot(
        teacher_attended,
        lax.all_gather(w_out_teacher, ("cam", "slab"), axis=0, tiled=True),
        preferred_element_type=jnp.float32,
    )
    targets = norm_rows(masked_resid.astype(jnp.float32) + projected).astype(jnp.bfloat16)
    devices = lax.axis_size(("cam", "slab"))
    capacity = 2 * masked_count // devices
    myself = lax.axis_index(("cam", "slab"))
    own_dest = lax.dynamic_index_in_dim(
        owners.reshape(devices, masked_count), myself, 0, keepdims=False
    )
    earlier = jnp.tril(jnp.ones((masked_count, masked_count), jnp.bool_), -1)
    same_owner = own_dest[:, None] == own_dest[None, :]
    order_rank = jnp.sum((same_owner & earlier).astype(jnp.int32), axis=1)
    slot_index = own_dest * capacity + order_rank
    slot_total = devices * capacity
    query_rows = pred_query[0]
    pred_width = query_rows.shape[1]
    full_query, full_key, full_value, full_out, full_proj = (
        lax.all_gather(w_query, ("cam", "slab"), axis=0, tiled=True),
        lax.all_gather(w_key, ("cam", "slab"), axis=0, tiled=True),
        lax.all_gather(w_value, ("cam", "slab"), axis=0, tiled=True),
        lax.all_gather(w_out, ("cam", "slab"), axis=0, tiled=True),
        lax.all_gather(w_proj, ("cam", "slab"), axis=0, tiled=True),
    )
    pred_head = pred_width // P_HEADS
    pred_heads = (
        jnp.dot(query_rows, full_query, preferred_element_type=jnp.float32)
        .astype(jnp.bfloat16)
        .reshape(masked_count, P_HEADS, pred_head)
    )
    start_state = empty_state(masked_count, P_HEADS, pred_head)
    context = lax.all_gather(pred_context[0], ("cam", "slab"), axis=0, tiled=True)
    context_keys = jnp.dot(context, full_key, preferred_element_type=jnp.float32)
    context_values = jnp.dot(context, full_value, preferred_element_type=jnp.float32)
    running_max, weight_sum, accumulated = attend_block(
        start_state,
        pred_heads,
        context_keys.astype(jnp.bfloat16),
        context_values.astype(jnp.bfloat16),
    )
    pred_attended = finish_heads(weight_sum, accumulated)
    pred_hidden = query_rows.astype(jnp.float32) + jnp.dot(
        pred_attended, full_out, preferred_element_type=jnp.float32
    )
    predicted = norm_rows(pred_hidden).astype(jnp.bfloat16)
    difference = jnp.dot(
        predicted, full_proj, preferred_element_type=jnp.float32
    ) - targets.astype(jnp.float32)
    sent = (
        jnp.zeros((slot_total, model_width), jnp.bfloat16)
        .at[slot_index]
        .set(difference.astype(jnp.bfloat16))
        .reshape(devices, capacity, model_width)
    )
    errors = lax.all_to_all(sent, ("cam", "slab"), split_axis=0, concat_axis=0, tiled=True)
    return errors.reshape(1, 1, slot_total, model_width)


def rows_dot(left, right):
    return lax.dot_general(
        left, right, (((1,), (1,)), ((), ())), preferred_element_type=jnp.float32
    )


def dot(left, right):
    return jnp.dot(left, right, preferred_element_type=jnp.float32)


def position():
    return lax.axis_index("cam"), lax.axis_index("slab")


def head_windows(head_count, head_size):
    windows = []
    for head in range(head_count):
        low, high = head * head_size, (head + 1) * head_size
        start = low // LANES * LANES
        windows.append((low, high, start, -(-high // LANES) * LANES))
    return windows


def inside(shape, start, low, high):
    lane = lax.broadcasted_iota(jnp.int32, shape, 1) + start
    return (lane >= low) & (lane < high)


def softmax_terms(scores, scale):
    peak = jnp.max(scores, axis=1, keepdims=True)
    terms = jnp.exp2((scores - peak) * scale)
    return terms.astype(jnp.bfloat16), jnp.sum(terms, axis=1, keepdims=True)


def slot_picker(key_row, owner, capacity, slot_total):
    shape = (2 * capacity, key_row.shape[1])
    row = lax.broadcasted_iota(jnp.int32, shape, 0)
    late = row >= capacity
    wanted = owner * capacity + row + jnp.where(late, slot_total - capacity, 0)
    return jnp.where(key_row == wanted, 1.0, 0.0).astype(jnp.bfloat16)


def pack_kernel(
    capacity, query, key, value, resid, mask, owners, wq, wk, wv, wo, wp, context,
    block0, block1, block2, block3, resid_rows, slot_keys, pack,
    stack, blocks, query_here, resid_here, mask_here, owners_here, done,
):
    cam, slab = position()
    tokens, width = key.shape
    masked = mask.shape[1]
    quarter = width // 8
    context_rows, pred_width = context.shape
    moves = [
        (mask, mask_here),
        (query, query_here),
        (key, stack.at[0:tokens]),
        (value, stack.at[tokens : 2 * tokens]),
        (resid, resid_here),
        (owners, owners_here),
    ]
    at = 0
    for part in (wq, wk, wv, wo, wp):
        moves.append((part, pack.at[:, at : at + part.shape[1]]))
        at += part.shape[1]
    moves.append((context, pack.at[0:context_rows, at:]))
    copies = [
        pltpu.make_async_copy(source, target, done.at[number])
        for number, (source, target) in enumerate(moves)
    ]
    for copy in copies:
        copy.start()
    pack[context_rows:, at:] = jnp.zeros((pack.shape[0] - context_rows, pred_width), jnp.bfloat16)
    token = lax.broadcasted_iota(jnp.int32, (tokens, masked), 0)
    for copy in copies[:4]:
        copy.wait()
    chosen = jnp.where(token == mask_here[...], 1.0, 0.0).T.astype(jnp.bfloat16)
    stack[2 * tokens :] = dot(chosen, query_here[...]).astype(jnp.bfloat16)
    row_total = stack.shape[0]
    pad = blocks.shape[2] - 2 * quarter
    for other in range(4):
        first = stack[:, other * quarter : (other + 1) * quarter]
        second = stack[:, (other + 4) * quarter : (other + 5) * quarter]
        blocks[other] = jnp.concatenate(
            [first, second, jnp.zeros((row_total, pad), jnp.bfloat16)], axis=1
        )
    for relation, out in enumerate((block0, block1, block2, block3)):
        out[...] = blocks[slab ^ relation]
    for copy in copies[4:]:
        copy.wait()
    resid_rows[...] = dot(chosen, resid_here[...]).astype(jnp.bfloat16)
    owners = owners_here
    listed = owners.shape[1]
    before = lax.broadcasted_iota(jnp.int32, (listed, listed), 0)
    after = lax.broadcasted_iota(jnp.int32, (listed, listed), 1)
    group = sum((before >= edge).astype(jnp.int32) for edge in range(masked, listed, masked))
    group_after = sum((after >= edge).astype(jnp.int32) for edge in range(masked, listed, masked))
    precedes = jnp.where((before < after) & (group == group_after), 1.0, 0.0)
    owner_row = owners[pl.ds(cam, 1), :]
    device = lax.broadcasted_iota(jnp.int32, (8, listed), 0)
    owned = jnp.where(device == owner_row, 1.0, 0.0)
    counted = dot(owned.astype(jnp.bfloat16), precedes.astype(jnp.bfloat16))
    rank = jnp.sum(owned * counted, axis=0, keepdims=True).astype(jnp.int32)
    lane = lax.broadcasted_iota(jnp.int32, (1, listed), 1)
    odd = ((lane >= masked) & (lane < 2 * masked)) | (lane >= 3 * masked)
    keys = owner_row * capacity + rank + jnp.where(odd, 8 * capacity, 0)
    slot_keys[0:1, :] = keys[:, 0 : 2 * masked]
    slot_keys[1:2, :] = keys[:, 2 * masked :]


def bundle_kernel(first, second, third, asked1, asked2, asked3, after, weights, contexts):
    rows = first.shape[0]
    for number, piece in enumerate((first, second, third)):
        weights[number * rows : (number + 1) * rows] = piece[...]
    rows = contexts.shape[0] // 3
    for number, asked in enumerate((asked1, asked2, asked3)):
        contexts[number * rows : (number + 1) * rows] = asked[asked.shape[0] - rows :]


def ask_kernel(
    capacity, slot_keys, own_rows, peer_rows, context, out0, out1, out2, out3, pair
):
    cam, slab = position()
    rows = own_rows.shape[0]
    core = slab % 2
    pair[pl.ds(pl.multiple_of(core * rows, rows), rows)] = own_rows[...]
    pair[pl.ds(pl.multiple_of((1 - core) * rows, rows), rows)] = peer_rows[...]
    key_row = slot_keys[pl.ds(slab // 2, 1), :]
    for relation, out in enumerate((out0, out1, out2, out3)):
        owner = (cam * 4 + slab) ^ (relation * 2)
        picker = slot_picker(key_row, owner, capacity, 8 * capacity)
        out[0 : 2 * capacity] = dot(picker, pair[...]).astype(jnp.bfloat16)
        if relation:
            out[2 * capacity :] = context[...]


def hold_kernel(pack, after, out):
    out[...] = pack[:, 0 : out.shape[1]]


def teacher_kernel(
    capacity, head_size, tokens, masked, slot_keys, block0, block1, block2, block3,
    own_core, peer_core, queries, keys, values, attended,
):
    cam, slab = position()
    for relation, block in enumerate((block0, block1, block2, block3)):
        other = slab ^ relation
        keys[relation * tokens : (relation + 1) * tokens] = block[0:tokens]
        values[relation * tokens : (relation + 1) * tokens] = block[tokens : 2 * tokens]
        queries[pl.ds(pl.multiple_of(other * masked, masked), masked)] = block[2 * tokens :]
    scale = math.log2(math.e) / math.sqrt(head_size)
    chunk = 2 * masked
    for half in range(2):
        rows = slice(half * chunk, (half + 1) * chunk)
        total = [jnp.zeros((chunk, LANES), jnp.float32) for _ in range(attended.shape[1] // LANES)]
        for low, high, start, stop in head_windows(4, head_size):
            window = inside((chunk, stop - start), start, low, high)
            picked = jnp.where(window, queries[rows, start:stop].astype(jnp.float32), 0.0)
            scores = rows_dot(picked.astype(jnp.bfloat16), keys[:, start:stop])
            terms, weight = softmax_terms(scores, scale)
            mixed = dot(terms, values[:, start:stop]) / weight
            mixed = jnp.where(window, mixed, 0.0)
            for tile in range(start // LANES, stop // LANES):
                total[tile] += mixed[:, tile * LANES - start : (tile + 1) * LANES - start]
        attended[rows] = jnp.concatenate(total, axis=1).astype(jnp.bfloat16)
    for flip, out in enumerate((own_core, peer_core)):
        for relation in range(4):
            owner = (cam * 4 + slab) ^ (relation * 2 + flip)
            for half in range(2):
                picker = slot_picker(slot_keys[half : half + 1, :], owner, capacity, 8 * capacity)
                at = (relation * 2 + half) * 2 * capacity
                out[at : at + 2 * capacity] = dot(
                    picker, attended[half * chunk : (half + 1) * chunk]
                ).astype(jnp.bfloat16)


def project_kernel(
    capacity, slot_keys, own_slots, peer_slots, w_own, w_cam, w_core, w_both, resid_own, resid_peer,
    out0, out1, out2, out3, weight, resid_pair, total,
):
    cam, slab = position()
    core, chip = slab % 2, slab // 2
    part, width = w_own.shape
    half = own_slots.shape[1]
    for base, same, crossed in ((0, w_own, w_cam), (half, w_core, w_both)):
        weight[pl.ds(pl.multiple_of(base + cam * part, 16), part)] = same[...]
        weight[pl.ds(pl.multiple_of(base + (1 - cam) * part, 16), part)] = crossed[...]
        weight[base + 2 * part : base + half] = jnp.zeros((half - 2 * part, width), jnp.bfloat16)
    rows = resid_own.shape[0]
    resid_pair[pl.ds(pl.multiple_of(core * rows, rows), rows)] = resid_own[...]
    resid_pair[pl.ds(pl.multiple_of((1 - core) * rows, rows), rows)] = resid_peer[...]
    key_row = slot_keys[pl.ds(chip, 1), :]
    block = out0.shape[0]
    for relation, out in ((3, out3), (2, out2), (1, out1), (0, out0)):
        at = relation * block
        total[...] = dot(own_slots[at : at + block], weight[0:half]) + dot(
            peer_slots[at : at + block], weight[half:]
        )
        owner = (cam * 4 + slab) ^ (relation * 2)
        picker = slot_picker(key_row, owner, capacity, 8 * capacity)
        own_rows = pl.ds(pl.multiple_of(chip * 2 * capacity, 8), 2 * capacity)
        total[own_rows] = total[own_rows] + dot(picker, resid_pair[...])
        out[...] = total[...].astype(jnp.bfloat16)


def predict_kernel(
    ask0, ask1, ask2, ask3, own_pack, first, second, third, peer_pack, peer_weights, peer_contexts,
    out, queries, weights, context,
):
    cam, slab = position()
    parity = lax.axis_index("clip") % 2
    rows, width = ask0.shape
    own = cam * 4 + slab
    part, wide = first.shape
    context_rows = peer_contexts.shape[0] // 3

    def place(source, piece):
        weights[pl.ds(pl.multiple_of(source * part, part), part)] = piece

    def place_context(source, piece):
        context[pl.ds(pl.multiple_of(source * context_rows, context_rows), context_rows)] = piece

    for flip, piece in enumerate((own_pack, peer_pack)):
        place(own ^ flip, piece[:, 0:wide])
        place_context(own ^ flip, piece[0:context_rows, wide:])
    for number, piece in enumerate((first, second, third)):
        relation = (1 + parity, 2 - parity, 3)[number] * 2
        place(own ^ relation, piece[...])
        place(own ^ (relation + 1), peer_weights[number * part : (number + 1) * part])
    for number, asked in enumerate((ask1, ask2, ask3)):
        relation = (number + 1) * 2
        place_context(own ^ relation, asked[rows:])
        place_context(
            own ^ (relation + 1),
            peer_contexts[number * context_rows : (number + 1) * context_rows],
        )
    for relation, asked in enumerate((ask0, ask1, ask2, ask3)):
        source = (own // 2) ^ relation
        queries[pl.ds(pl.multiple_of(source * rows, rows), rows)] = asked[0:rows]
    head_size = width // P_HEADS
    scale = math.log2(math.e) / math.sqrt(head_size)
    asked = dot(queries[...], weights[:, 0:width]).astype(jnp.bfloat16)
    seen_keys = dot(context[...], weights[:, width : 2 * width]).astype(jnp.bfloat16)
    seen_values = dot(context[...], weights[:, 2 * width : 3 * width]).astype(jnp.bfloat16)
    total = [jnp.zeros((asked.shape[0], LANES), jnp.float32) for _ in range(width // LANES)]
    for low, high, start, stop in head_windows(P_HEADS, head_size):
        window = inside((asked.shape[0], stop - start), start, low, high)
        picked = jnp.where(window, asked[:, start:stop].astype(jnp.float32), 0.0)
        scores = rows_dot(picked.astype(jnp.bfloat16), seen_keys[:, start:stop])
        terms, weight = softmax_terms(scores, scale)
        mixed = dot(terms, seen_values[:, start:stop]) / weight
        total[start // LANES] += jnp.where(window, mixed, 0.0)
    attended = jnp.concatenate(total, axis=1).astype(jnp.bfloat16)
    hidden = queries[...].astype(jnp.float32) + dot(attended, weights[:, 3 * width : 4 * width])
    predicted = norm_rows(hidden).astype(jnp.bfloat16)
    out[...] = dot(predicted, weights[:, 4 * width :])


def finish_kernel(capacity, masked, owners, predicted, part0, part1, part2, part3, out):
    cam, slab = position()
    rows = part0.shape[0]
    for flip, (near, far) in enumerate(((part0, part1), (part2, part3))):
        camera = cam ^ flip
        at = pl.ds(pl.multiple_of(camera * rows, rows), rows)
        summed = near[...].astype(jnp.float32) + far[...].astype(jnp.float32)
        shape = (rows, owners.shape[1])
        row = lax.broadcasted_iota(jnp.int32, shape, 0)
        lane = lax.broadcasted_iota(jnp.int32, shape, 1)
        listed = owners[pl.ds(camera, 1), :] == cam * 4 + slab
        same = jnp.zeros(shape, jnp.bool_)
        for group in range(4):
            same = same | (
                (row >= group * capacity)
                & (row < (group + 1) * capacity)
                & (lane >= group * masked)
                & (lane < (group + 1) * masked)
            )
        count = jnp.sum(jnp.where(same & listed, 1.0, 0.0), axis=1, keepdims=True)
        order = lax.broadcasted_iota(jnp.int32, (rows, 1), 0)
        order = order - sum(
            jnp.where(order >= group * capacity, capacity, 0) for group in range(1, 4)
        )
        filled = order.astype(jnp.float32) < count
        goal = norm_rows(summed).astype(jnp.bfloat16).astype(jnp.float32)
        out[at] = jnp.where(filled, predicted[at] - goal, 0.0).astype(jnp.bfloat16)


def call(kernel, outs, scratch, *args, far=0, after=0, light=False):
    shapes = tuple(jax.ShapeDtypeStruct(shape, dtype) for shape, dtype in outs)
    near = pl.BlockSpec(memory_space=pltpu.VMEM)
    scratch_shapes = [pltpu.VMEM(shape, dtype) for shape, dtype in scratch]
    if far:
        scratch_shapes.append(pltpu.SemaphoreType.DMA((far,)))
        args = [pltpu.with_memory_space_constraint(arg, pltpu.HBM) for arg in args[:far]] + list(args[far:])
    return pl.pallas_call(
        kernel,
        out_shape=shapes,
        in_specs=[pl.BlockSpec(memory_space=pltpu.HBM)] * far
        + [near] * (len(args) - far - after)
        + [pl.BlockSpec(memory_space=pl.ANY)] * after,
        out_specs=tuple(near for _ in outs),
        scratch_shapes=scratch_shapes,
        compiler_params=pltpu.CompilerParams(vmem_limit_bytes=40 * 2**20),
        cost_estimate=pl.CostEstimate(flops=1, bytes_accessed=1, transcendentals=0) if light else None,
    )(*args)


def send(rows, flip):
    return lax.ppermute(rows, ("cam", "slab"), [(source, source ^ flip) for source in range(8)])


def send_alternating(rows, clips, even, odd):
    pairs = [
        (clip * 8 + source, clip * 8 + (source ^ (odd if clip % 2 else even)))
        for clip in range(clips)
        for source in range(8)
    ]
    return lax.ppermute(rows, ("clip", "cam", "slab"), pairs)


def swap_clips(rows, clips):
    return lax.ppermute(rows, "clip", [(clip, clip ^ 1) for clip in range(clips)])


def paired_shards(
    t_query, t_key, t_value, t_resid, w_out_teacher, pred_query, pred_context,
    w_query, w_key, w_value, w_out, w_proj, mask_list, owners,
):
    bf16, f32 = jnp.bfloat16, jnp.float32
    tokens, width = t_key.shape[1:]
    masked, pred_width = pred_query.shape[1:]
    capacity = masked // 4
    quarter = width // 8
    head_size = width // HEADS
    context_rows = pred_context.shape[1]
    padded = -(-2 * quarter // LANES) * LANES
    block_rows = 2 * tokens + masked
    block = ((block_rows, padded), bf16)
    weight_rows = w_query.shape[0]
    weight_width = 4 * pred_width + w_proj.shape[1]
    pack_width = weight_width + pred_width
    peer_query = send(pred_query[0], 1)
    w_core = send(w_out_teacher, 1)
    w_cam = send(w_out_teacher, 4)
    block0, block1, block2, block3, resid_rows, slot_keys, pack = call(
        functools.partial(pack_kernel, capacity),
        [block] * 4
        + [((masked, width), bf16), ((2, 2 * masked), jnp.int32), ((weight_rows, pack_width), bf16)],
        [
            ((block_rows, width), bf16), ((4, block_rows, padded), bf16), ((tokens, width), bf16),
            ((tokens, width), bf16), (mask_list.shape, jnp.int32), (owners.shape, jnp.int32),
        ],
        t_query[0], t_key[0], t_value[0], t_resid[0], mask_list, owners,
        w_query, w_key, w_value, w_out, w_proj, pred_context[0], far=12,
    )
    other2, other3, other1 = send(block2, 2), send(block3, 3), send(block1, 1)
    w_both = send(w_cam, 1)
    peer_resid = send(resid_rows, 1)
    ask = ((2 * capacity + context_rows, pred_width), bf16)
    ask0, ask1, ask2, ask3 = call(
        functools.partial(ask_kernel, capacity),
        [((2 * capacity, pred_width), bf16), ask, ask, ask],
        [((2 * masked, pred_width), bf16)],
        slot_keys, pred_query[0], peer_query, pred_context[0],
    )
    asked1, asked2, asked3 = send(ask1, 2), send(ask2, 4), send(ask3, 6)
    peer_pack = send(pack, 1)
    clips = lax.axis_size("clip")
    shard = ((weight_rows, weight_width), bf16)
    (held,) = call(hold_kernel, [shard], [], pack, other2, after=1, light=True)
    first = send_alternating(held, clips, 2, 4)
    third = send_alternating(first, clips, 4, 2)
    second = swap_clips(first, clips)
    slots = ((16 * capacity, padded), bf16)
    own_slots, away_slots = call(
        functools.partial(teacher_kernel, capacity, head_size, tokens, masked),
        [slots, slots],
        [
            ((4 * masked, padded), bf16), ((4 * tokens, padded), bf16), ((4 * tokens, padded), bf16),
            ((4 * masked, padded), bf16),
        ],
        slot_keys, block0, other1, other2, other3,
    )
    peer_slots = send(away_slots, 1)
    part = ((4 * capacity, width), bf16)
    part0, part1, part2, part3 = call(
        functools.partial(project_kernel, capacity),
        [part] * 4,
        [((2 * padded, width), bf16), ((2 * masked, width), bf16), ((4 * capacity, width), f32)],
        slot_keys, own_slots, peer_slots, w_out_teacher, w_cam, w_core, w_both, resid_rows, peer_resid,
    )
    far1, far2, far3 = send(part1, 2), send(part2, 4), send(part3, 6)
    bundle, contexts = call(
        bundle_kernel,
        [((3 * weight_rows, weight_width), bf16), ((3 * context_rows, pred_width), bf16)],
        [],
        first, second, third, asked1, asked2, asked3, part0,
        after=1, light=True,
    )
    (predicted,) = call(
        predict_kernel,
        [((8 * capacity, width), f32)],
        [
            ((8 * capacity, pred_width), bf16), ((8 * weight_rows, weight_width), bf16),
            ((8 * context_rows, pred_width), bf16),
        ],
        ask0, asked1, asked2, asked3, pack, first, second, third, peer_pack, send(bundle, 1),
        send(contexts, 1),
        light=True,
    )
    (errors,) = call(
        functools.partial(finish_kernel, capacity, masked),
        [((8 * capacity, width), bf16)],
        [],
        owners, predicted, part0, far1, far2, far3,
    )
    return errors[None, None]


def solution(mesh):
    placed = (
        P(("clip", "cam"), "slab", None),
        P(("clip", "cam"), "slab", None),
        P(("clip", "cam"), "slab", None),
        P(("clip", "cam"), "slab", None),
        P(("cam", "slab"), None),
        P(("clip", "cam"), "slab", None),
        P(("clip", "cam"), "slab", None),
        P(("cam", "slab"), None),
        P(("cam", "slab"), None),
        P(("cam", "slab"), None),
        P(("cam", "slab"), None),
        P(("cam", "slab"), None),
        P(("clip", "cam"), "slab"),
        P("clip", None),
    )
    small = (mesh.shape["cam"], mesh.shape["slab"]) == (2, 4) and mesh.shape["clip"] % 2 == 0
    return jax.shard_map(
        paired_shards if small else shards,
        mesh=mesh,
        in_specs=placed,
        out_specs=P(("clip", "cam"), "slab", None, None),
        check_vma=False,
    )
```

```python
import functools
import math

import jax
import jax.numpy as jnp
from jax import lax
from jax.experimental import pallas as pl
from jax.experimental.pallas import tpu as pltpu
from jax.sharding import PartitionSpec as P

HEADS = 16
P_HEADS = 12
LANES = 128


def norm_rows(values_in):
    average = jnp.mean(values_in, axis=-1, keepdims=True)
    centered = values_in - average
    variance = jnp.mean(centered * centered, axis=-1, keepdims=True)
    return centered * lax.rsqrt(variance + 1e-06)


def empty_state(row_count, head_count, head_size):
    return (
        jnp.full((row_count, head_count), -1e30, jnp.float32),
        jnp.zeros((row_count, head_count), jnp.float32),
        jnp.zeros((row_count, head_count, head_size), jnp.float32),
    )


def attend_block(state_now, query_heads, key_rows, value_rows):
    head_count = query_heads.shape[1]
    head_size = query_heads.shape[2]
    running_max, weight_sum, accumulated = state_now
    for offset in range(0, key_rows.shape[0], 512):
        key_block = key_rows[offset : offset + 512].reshape(-1, head_count, head_size)
        value_block = value_rows[offset : offset + 512].reshape(-1, head_count, head_size)
        scores = jnp.einsum(
            "rhd,khd->rhk", query_heads, key_block, preferred_element_type=jnp.float32
        ) / math.sqrt(head_size)
        new_max = jnp.maximum(running_max, jnp.max(scores, axis=2))
        rescale = jnp.exp(running_max - new_max)
        exponent = jnp.exp(scores - new_max[:, :, None])
        weight_sum = weight_sum * rescale + jnp.sum(exponent, axis=2)
        accumulated = accumulated * rescale[:, :, None] + jnp.einsum(
            "rhk,khd->rhd",
            exponent.astype(jnp.bfloat16),
            value_block,
            preferred_element_type=jnp.float32,
        )
        running_max = new_max
    return (running_max, weight_sum, accumulated)


def finish_heads(weight_sum, accumulated):
    mixed = accumulated / weight_sum[:, :, None]
    return mixed.reshape(mixed.shape[0], -1).astype(jnp.bfloat16)


def shards(
    t_query,
    t_key,
    t_value,
    t_resid,
    w_out_teacher,
    pred_query,
    pred_context,
    w_query,
    w_key,
    w_value,
    w_out,
    w_proj,
    mask_list,
    owners,
):
    model_width = t_query.shape[2]
    head_size = model_width // HEADS
    local_rows = mask_list[0]
    masked_count = local_rows.shape[0]
    masked_query = jnp.take(t_query[0], local_rows, axis=0)
    masked_resid = jnp.take(t_resid[0], local_rows, axis=0)
    query_heads = masked_query.reshape(masked_count, HEADS, head_size)
    pieces = (
        lax.all_gather(t_key[0], "slab", axis=0, tiled=True),
        lax.all_gather(t_value[0], "slab", axis=0, tiled=True),
    )
    running_max, weight_sum, accumulated = attend_block(
        empty_state(masked_count, HEADS, head_size), query_heads, pieces[0], pieces[1]
    )
    teacher_attended = finish_heads(weight_sum, accumulated)
    projected = jnp.dot(
        teacher_attended,
        lax.all_gather(w_out_teacher, ("cam", "slab"), axis=0, tiled=True),
        preferred_element_type=jnp.float32,
    )
    targets = norm_rows(masked_resid.astype(jnp.float32) + projected).astype(jnp.bfloat16)
    devices = lax.axis_size(("cam", "slab"))
    capacity = 2 * masked_count // devices
    myself = lax.axis_index(("cam", "slab"))
    own_dest = lax.dynamic_index_in_dim(
        owners.reshape(devices, masked_count), myself, 0, keepdims=False
    )
    earlier = jnp.tril(jnp.ones((masked_count, masked_count), jnp.bool_), -1)
    same_owner = own_dest[:, None] == own_dest[None, :]
    order_rank = jnp.sum((same_owner & earlier).astype(jnp.int32), axis=1)
    slot_index = own_dest * capacity + order_rank
    slot_total = devices * capacity
    query_rows = pred_query[0]
    pred_width = query_rows.shape[1]
    full_query, full_key, full_value, full_out, full_proj = (
        lax.all_gather(w_query, ("cam", "slab"), axis=0, tiled=True),
        lax.all_gather(w_key, ("cam", "slab"), axis=0, tiled=True),
        lax.all_gather(w_value, ("cam", "slab"), axis=0, tiled=True),
        lax.all_gather(w_out, ("cam", "slab"), axis=0, tiled=True),
        lax.all_gather(w_proj, ("cam", "slab"), axis=0, tiled=True),
    )
    pred_head = pred_width // P_HEADS
    pred_heads = (
        jnp.dot(query_rows, full_query, preferred_element_type=jnp.float32)
        .astype(jnp.bfloat16)
        .reshape(masked_count, P_HEADS, pred_head)
    )
    start_state = empty_state(masked_count, P_HEADS, pred_head)
    context = lax.all_gather(pred_context[0], ("cam", "slab"), axis=0, tiled=True)
    context_keys = jnp.dot(context, full_key, preferred_element_type=jnp.float32)
    context_values = jnp.dot(context, full_value, preferred_element_type=jnp.float32)
    running_max, weight_sum, accumulated = attend_block(
        start_state,
        pred_heads,
        context_keys.astype(jnp.bfloat16),
        context_values.astype(jnp.bfloat16),
    )
    pred_attended = finish_heads(weight_sum, accumulated)
    pred_hidden = query_rows.astype(jnp.float32) + jnp.dot(
        pred_attended, full_out, preferred_element_type=jnp.float32
    )
    predicted = norm_rows(pred_hidden).astype(jnp.bfloat16)
    difference = jnp.dot(
        predicted, full_proj, preferred_element_type=jnp.float32
    ) - targets.astype(jnp.float32)
    sent = (
        jnp.zeros((slot_total, model_width), jnp.bfloat16)
        .at[slot_index]
        .set(difference.astype(jnp.bfloat16))
        .reshape(devices, capacity, model_width)
    )
    errors = lax.all_to_all(sent, ("cam", "slab"), split_axis=0, concat_axis=0, tiled=True)
    return errors.reshape(1, 1, slot_total, model_width)


def rows_dot(left, right):
    return lax.dot_general(
        left, right, (((1,), (1,)), ((), ())), preferred_element_type=jnp.float32
    )


def dot(left, right):
    return jnp.dot(left, right, preferred_element_type=jnp.float32)


def position():
    return lax.axis_index("cam"), lax.axis_index("slab")


def head_windows(head_count, head_size):
    windows = []
    for head in range(head_count):
        low, high = head * head_size, (head + 1) * head_size
        start = low // LANES * LANES
        windows.append((low, high, start, -(-high // LANES) * LANES))
    return windows


def inside(shape, start, low, high):
    lane = lax.broadcasted_iota(jnp.int32, shape, 1) + start
    return (lane >= low) & (lane < high)


def softmax_terms(scores, scale):
    peak = jnp.max(scores, axis=1, keepdims=True)
    terms = jnp.exp2((scores - peak) * scale)
    return terms.astype(jnp.bfloat16), jnp.sum(terms, axis=1, keepdims=True)


def slot_picker(key_row, owner, capacity, slot_total):
    shape = (2 * capacity, key_row.shape[1])
    row = lax.broadcasted_iota(jnp.int32, shape, 0)
    late = row >= capacity
    wanted = owner * capacity + row + jnp.where(late, slot_total - capacity, 0)
    return jnp.where(key_row == wanted, 1.0, 0.0).astype(jnp.bfloat16)


def pack_kernel(
    capacity, query, key, value, resid, mask, owners, wq, wk, wv, wo, wp, asks, context, w_far,
    block0, block2, block3, resid_rows, slot_keys, pack, message, w_here,
    stack, blocks, query_here, resid_here, mask_here, owners_here, done,
):
    cam, slab = position()
    tokens, width = key.shape
    masked, pred_width = asks.shape
    quarter = width // 8
    context_rows = context.shape[0]
    row_total = stack.shape[0]
    part_rows, half = w_far.shape[0], masked // 2
    moves = [
        (mask, mask_here),
        (query, query_here),
        (key, stack.at[0:tokens]),
        (value, stack.at[tokens : 2 * tokens]),
        (resid, resid_here),
        (owners, owners_here),
        (w_far, w_here.at[0:part_rows]),
        (asks, block2.at[row_total : row_total + masked]),
        (context, block2.at[row_total + masked :]),
        (asks.at[0:half], w_here.at[part_rows:, 0:pred_width]),
        (asks.at[half:], w_here.at[part_rows:, pred_width : 2 * pred_width]),
        (
            context,
            w_here.at[part_rows : part_rows + context_rows, 2 * pred_width : 3 * pred_width],
        ),
    ]
    at = 0
    for part in (wq, wk, wv, wo, wp):
        moves.append((part, pack.at[:, at : at + part.shape[1]]))
        at += part.shape[1]
    copies = [
        pltpu.make_async_copy(source, target, done.at[number])
        for number, (source, target) in enumerate(moves)
    ]
    for copy in copies:
        copy.start()
    w_here[part_rows:, 3 * pred_width :] = jnp.zeros((half, width - 3 * pred_width), jnp.bfloat16)
    w_here[part_rows + context_rows :, 2 * pred_width : 3 * pred_width] = jnp.zeros(
        (half - context_rows, pred_width), jnp.bfloat16
    )
    token = lax.broadcasted_iota(jnp.int32, (tokens, masked), 0)
    for copy in copies[:4]:
        copy.wait()
    chosen = jnp.where(token == mask_here[...], 1.0, 0.0).T.astype(jnp.bfloat16)
    stack[2 * tokens :] = dot(chosen, query_here[...]).astype(jnp.bfloat16)
    pad = blocks.shape[2] - 2 * quarter
    for other in range(4):
        first = stack[:, other * quarter : (other + 1) * quarter]
        second = stack[:, (other + 4) * quarter : (other + 5) * quarter]
        blocks[other] = jnp.concatenate(
            [first, second, jnp.zeros((row_total, pad), jnp.bfloat16)], axis=1
        )
    for relation, out in ((0, block0), (2, block2), (3, block3)):
        out[0:row_total] = blocks[slab ^ relation]
    core_block = blocks.at[slab ^ 1]
    for copy in copies[4:]:
        copy.wait()
    resid_rows[...] = dot(chosen, resid_here[...]).astype(jnp.bfloat16)
    base = w_here.shape[0]
    message[0:base] = w_here[...]
    message[base : base + masked] = resid_rows[...]
    base += masked
    count = pack.shape[0]
    message[base + 2 * count : base + 3 * count] = jnp.zeros((count, width), jnp.bfloat16)
    for low in range(0, at, width):
        high = min(low + width, at)
        message[base : base + count, 0 : high - low] = pack[:, low:high]
        base += count
    message[base:] = jnp.zeros((tokens, width), jnp.bfloat16)
    for number in range(3):
        low, high = number * tokens, min((number + 1) * tokens, row_total)
        lanes = slice(number * core_block.shape[1], (number + 1) * core_block.shape[1])
        message[base : base + high - low, lanes] = core_block[low:high]
    listed = owners.shape[1]
    before = lax.broadcasted_iota(jnp.int32, (listed, listed), 0)
    after = lax.broadcasted_iota(jnp.int32, (listed, listed), 1)
    group = sum((before >= edge).astype(jnp.int32) for edge in range(masked, listed, masked))
    group_after = sum((after >= edge).astype(jnp.int32) for edge in range(masked, listed, masked))
    precedes = jnp.where((before < after) & (group == group_after), 1.0, 0.0)
    precedes = precedes.astype(jnp.bfloat16)
    lane = lax.broadcasted_iota(jnp.int32, (1, listed), 1)
    odd = ((lane >= masked) & (lane < 2 * masked)) | (lane >= 3 * masked)
    device = lax.broadcasted_iota(jnp.int32, (8, listed), 0)
    for camera in range(2):
        owner_row = owners_here[camera : camera + 1, :]
        owned = jnp.where(device == owner_row, 1.0, 0.0)
        counted = dot(owned.astype(jnp.bfloat16), precedes)
        rank = jnp.sum(owned * counted, axis=0, keepdims=True).astype(jnp.int32)
        keys = owner_row * capacity + rank + jnp.where(odd, 8 * capacity, 0)
        slot_keys[2 * camera : 2 * camera + 1, :] = keys[:, 0 : 2 * masked]
        slot_keys[2 * camera + 1 : 2 * camera + 2, :] = keys[:, 2 * masked :]


def hold_kernel(base, pack, block, message, held, passed):
    core = lax.axis_index("slab") % 2
    rows, wide = pack.shape
    width = message.shape[1]
    held[pl.ds(pl.multiple_of(core * rows, rows), rows)] = pack[...]
    other = pl.ds(pl.multiple_of((1 - core) * rows, rows), rows)
    for number, low in enumerate(range(0, wide, width)):
        high = min(low + width, wide)
        at = base + number * rows
        held[other, low:high] = message[at : at + rows, 0 : high - low]
    passed[...] = block[block.shape[0] - passed.shape[0] :]


def bundle_kernel(first, near, far, beside, after, out, forward):
    rows, wide = first.shape
    core = lax.axis_index("slab") % 2
    part = forward.shape[0]
    forward[...] = first[pl.ds(pl.multiple_of(core * part, part), part)]
    out[:, 0:wide] = first[...]
    asked_rows, width = far.shape
    rest = asked_rows - rows
    at = wide + 3 * width
    for number, piece in enumerate((near.at[near.shape[0] - asked_rows :], far)):
        out[:, wide + number * width : wide + (number + 1) * width] = piece[0:rows]
        out[number * rest : (number + 1) * rest, at:] = piece[rows:]
    base = beside.shape[0] - rows // 2
    out[0 : rows // 2, at - width : at] = beside[base:, 0:width]
    out[rows // 2 :, at - width : at] = beside[base:, width : 2 * width]
    out[2 * rest : 3 * rest, at:] = beside[base : base + rest, 2 * width : 3 * width]
    if 3 * rest < rows:
        out[3 * rest :, at:] = jnp.zeros((rows - 3 * rest, width), jnp.bfloat16)


def split_kernel(piece, after, left, right):
    left[...] = piece[:, 0 : left.shape[1]]
    right[...] = piece[:, left.shape[1] :]


def teacher_kernel(
    capacity, head_size, tokens, masked, slot_keys, block0, message, block2, block3, w_cam,
    own_core, peer_core, w_pass, queries, keys, values, attended,
):
    cam, slab = position()
    w_pass[...] = w_cam[0 : w_pass.shape[0]]
    wide, base = keys.shape[1], message.shape[0] - tokens
    pieces = [message.at[base:, number * wide : (number + 1) * wide] for number in range(3)]
    for relation, block in enumerate((block0, None, block2, block3)):
        if relation == 1:
            key_part, value_part, query_part = pieces
            query_part = query_part.at[0:masked]
        else:
            key_part, value_part = block.at[0:tokens], block.at[tokens : 2 * tokens]
            query_part = block.at[2 * tokens : 2 * tokens + masked]
        keys[relation * tokens : (relation + 1) * tokens] = key_part[...]
        values[relation * tokens : (relation + 1) * tokens] = value_part[...]
        start = pl.multiple_of((slab ^ relation) * masked, masked)
        queries[pl.ds(start, masked)] = query_part[...]
    scale = math.log2(math.e) / math.sqrt(head_size)
    chunk = 2 * masked
    for half in range(2):
        rows = slice(half * chunk, (half + 1) * chunk)
        total = [jnp.zeros((chunk, LANES), jnp.float32) for _ in range(attended.shape[1] // LANES)]
        for low, high, start, stop in head_windows(4, head_size):
            window = inside((chunk, stop - start), start, low, high)
            picked = jnp.where(window, queries[rows, start:stop].astype(jnp.float32), 0.0)
            scores = rows_dot(picked.astype(jnp.bfloat16), keys[:, start:stop])
            terms, weight = softmax_terms(scores, scale)
            mixed = dot(terms, values[:, start:stop]) / weight
            mixed = jnp.where(window, mixed, 0.0)
            for tile in range(start // LANES, stop // LANES):
                total[tile] += mixed[:, tile * LANES - start : (tile + 1) * LANES - start]
        attended[rows] = jnp.concatenate(total, axis=1).astype(jnp.bfloat16)
    for flip, out in enumerate((own_core, peer_core)):
        for relation in range(4):
            owner = (cam * 4 + slab) ^ (relation * 2 + flip)
            for half in range(2):
                picker = slot_picker(slot_keys[pl.ds(2 * cam + half, 1), :], owner, capacity, 8 * capacity)
                at = (relation * 2 + half) * 2 * capacity
                out[at : at + 2 * capacity] = dot(
                    picker, attended[half * chunk : (half + 1) * chunk]
                ).astype(jnp.bfloat16)


def project_kernel(
    capacity, slot_keys, own_slots, peer_slots, w_own, w_cam, w_core, w_both, resid_own,
    out0, out1, out2, out3, weight, resid_pair, total,
):
    cam, slab = position()
    core, chip = slab % 2, slab // 2
    width = w_own.shape[1]
    part = width // 8
    half = own_slots.shape[1]
    for base, same, crossed in ((0, w_own, w_cam), (half, w_core, w_both)):
        weight[pl.ds(pl.multiple_of(base + cam * part, 16), part)] = same[0:part]
        weight[pl.ds(pl.multiple_of(base + (1 - cam) * part, 16), part)] = crossed[0:part]
        weight[base + 2 * part : base + half] = jnp.zeros((half - 2 * part, width), jnp.bfloat16)
    rows = resid_own.shape[0]
    resid_pair[pl.ds(pl.multiple_of(core * rows, rows), rows)] = resid_own[...]
    resid_pair[pl.ds(pl.multiple_of((1 - core) * rows, rows), rows)] = w_core[
        w_own.shape[0] : w_own.shape[0] + rows
    ]
    key_row = slot_keys[pl.ds(2 * cam + chip, 1), :]
    block = out0.shape[0]
    for relation, out in ((3, out3), (2, out2), (1, out1), (0, out0)):
        at = relation * block
        total[...] = dot(own_slots[at : at + block], weight[0:half]) + dot(
            peer_slots[at : at + block], weight[half:]
        )
        owner = (cam * 4 + slab) ^ (relation * 2)
        picker = slot_picker(key_row, owner, capacity, 8 * capacity)
        own_rows = pl.ds(pl.multiple_of(chip * 2 * capacity, 8), 2 * capacity)
        total[own_rows] = total[own_rows] + dot(picker, resid_pair[...])
        out[...] = total[...].astype(jnp.bfloat16)


def predict_kernel(
    capacity, part_rows, slot_keys, w_own, w_core, w_cam, near, far,
    held, first, third, peer_left, peer_right, peers, out,
    queries, weights, context, asks,
):
    cam, slab = position()
    core = slab % 2
    own = cam * 4 + slab
    part, wide = third.shape
    width = far.shape[1]
    context_rows = context.shape[0] // 8
    masked = asks.shape[0] // 8
    half = masked // 2

    def place(source, piece):
        weights[pl.ds(pl.multiple_of(source * part, part), part)] = piece

    def place_context(source, piece):
        context[pl.ds(pl.multiple_of(source * context_rows, context_rows), context_rows)] = piece

    pair = 2 * part
    chip = own - core
    along, across = jnp.where(core == 0, 2, 4), jnp.where(core == 0, 4, 2)
    for source, piece in (
        (chip, held.at[0:pair]),
        (chip ^ along, first.at[0:pair]),
        (chip ^ across, peers.at[0:pair, 0:wide]),
    ):
        weights[pl.ds(pl.multiple_of(source * part, part), pair)] = piece[...]
    place(own ^ 6, third[...])
    last = pl.ds(pl.multiple_of((own ^ 7) * part, part), part)
    weights[last, 0 : peer_left.shape[1]] = peer_left[...]
    weights[last, peer_left.shape[1] :] = peer_right[...]
    for flip, piece in ((0, w_own), (1, w_core), (4, w_cam)):
        source = own ^ flip
        for number in range(2):
            start = pl.multiple_of(source * masked + number * half, half)
            asks[pl.ds(start, half)] = piece[part_rows : part_rows + half, number * width : (number + 1) * width]
        place_context(
            source, piece[part_rows : part_rows + context_rows, 2 * width : 3 * width]
        )
    base = near.shape[0] - masked - context_rows
    at = wide + 3 * width
    pieces = [(2, near.at[base : base + masked], near.at[base + masked :])]
    pieces.append((6, far.at[0:masked], far.at[masked:]))
    for number, flip in enumerate((3, 7, 5)):
        rows = peers.at[:, wide + number * width : wide + (number + 1) * width]
        pieces.append((flip, rows, peers.at[number * context_rows : (number + 1) * context_rows, at:]))
    for flip, rows, last in pieces:
        source = own ^ flip
        asks[pl.ds(pl.multiple_of(source * masked, masked), masked)] = rows[...]
        place_context(source, last[...])
    for chip in range(4):
        picker = slot_picker(slot_keys[chip : chip + 1, :], own, capacity, 8 * capacity)
        queries[chip * 2 * capacity : (chip + 1) * 2 * capacity] = dot(
            picker, asks[chip * 2 * masked : (chip + 1) * 2 * masked]
        ).astype(jnp.bfloat16)
    head_size = width // P_HEADS
    scale = math.log2(math.e) / math.sqrt(head_size)
    asked = dot(queries[...], weights[:, 0:width]).astype(jnp.bfloat16)
    seen_keys = dot(context[...], weights[:, width : 2 * width]).astype(jnp.bfloat16)
    seen_values = dot(context[...], weights[:, 2 * width : 3 * width]).astype(jnp.bfloat16)
    total = [jnp.zeros((asked.shape[0], LANES), jnp.float32) for _ in range(width // LANES)]
    for low, high, start, stop in head_windows(P_HEADS, head_size):
        window = inside((asked.shape[0], stop - start), start, low, high)
        picked = jnp.where(window, asked[:, start:stop].astype(jnp.float32), 0.0)
        scores = rows_dot(picked.astype(jnp.bfloat16), seen_keys[:, start:stop])
        terms, weight = softmax_terms(scores, scale)
        mixed = dot(terms, seen_values[:, start:stop]) / weight
        total[start // LANES] += jnp.where(window, mixed, 0.0)
    attended = jnp.concatenate(total, axis=1).astype(jnp.bfloat16)
    hidden = queries[...].astype(jnp.float32) + dot(attended, weights[:, 3 * width : 4 * width])
    predicted = norm_rows(hidden).astype(jnp.bfloat16)
    out[...] = dot(predicted, weights[:, 4 * width :])


def finish_kernel(capacity, masked, owners, predicted, part0, part1, part2, part3, out):
    cam, slab = position()
    rows = part0.shape[0]
    for flip, (near, far) in enumerate(((part0, part1), (part2, part3))):
        camera = cam ^ flip
        at = pl.ds(pl.multiple_of(camera * rows, rows), rows)
        summed = near[...].astype(jnp.float32) + far[...].astype(jnp.float32)
        shape = (rows, owners.shape[1])
        row = lax.broadcasted_iota(jnp.int32, shape, 0)
        lane = lax.broadcasted_iota(jnp.int32, shape, 1)
        listed = owners[pl.ds(camera, 1), :] == cam * 4 + slab
        same = jnp.zeros(shape, jnp.bool_)
        for group in range(4):
            same = same | (
                (row >= group * capacity)
                & (row < (group + 1) * capacity)
                & (lane >= group * masked)
                & (lane < (group + 1) * masked)
            )
        count = jnp.sum(jnp.where(same & listed, 1.0, 0.0), axis=1, keepdims=True)
        order = lax.broadcasted_iota(jnp.int32, (rows, 1), 0)
        order = order - sum(
            jnp.where(order >= group * capacity, capacity, 0) for group in range(1, 4)
        )
        filled = order.astype(jnp.float32) < count
        goal = norm_rows(summed).astype(jnp.bfloat16).astype(jnp.float32)
        out[at] = jnp.where(filled, predicted[at] - goal, 0.0).astype(jnp.bfloat16)


def call(kernel, outs, scratch, *args, far=0, copies=0, after=0):
    shapes = tuple(jax.ShapeDtypeStruct(shape, dtype) for shape, dtype in outs)
    near = pl.BlockSpec(memory_space=pltpu.VMEM)
    scratch_shapes = [pltpu.VMEM(shape, dtype) for shape, dtype in scratch]
    if far:
        scratch_shapes.append(pltpu.SemaphoreType.DMA((copies,)))
        args = [pltpu.with_memory_space_constraint(arg, pltpu.HBM) for arg in args[:far]] + list(args[far:])
    return pl.pallas_call(
        kernel,
        out_shape=shapes,
        in_specs=[pl.BlockSpec(memory_space=pltpu.HBM)] * far
        + [near] * (len(args) - far - after)
        + [pl.BlockSpec(memory_space=pl.ANY)] * after,
        out_specs=tuple(near for _ in outs),
        scratch_shapes=scratch_shapes,
        compiler_params=pltpu.CompilerParams(vmem_limit_bytes=40 * 2**20),
    )(*args)


def send(rows, flip):
    return lax.ppermute(rows, ("cam", "slab"), [(source, source ^ flip) for source in range(8)])


def send_by_core(rows, even, odd):
    pairs = [(source, source ^ (odd if source % 2 else even)) for source in range(8)]
    return lax.ppermute(rows, ("cam", "slab"), pairs)


def paired_shards(
    t_query, t_key, t_value, t_resid, w_out_teacher, pred_query, pred_context,
    w_query, w_key, w_value, w_out, w_proj, mask_list, owners,
):
    bf16, f32 = jnp.bfloat16, jnp.float32
    tokens, width = t_key.shape[1:]
    masked, pred_width = pred_query.shape[1:]
    capacity = masked // 4
    quarter = width // 8
    head_size = width // HEADS
    context_rows = pred_context.shape[1]
    padded = -(-2 * quarter // LANES) * LANES
    block_rows = 2 * tokens + masked
    block = ((block_rows, padded), bf16)
    weight_rows = w_query.shape[0]
    weight_width = 4 * pred_width + w_proj.shape[1]
    asked_rows = masked + context_rows
    message_rows = quarter + masked // 2 + masked + tokens - weight_width // -width * weight_rows
    shard = ((weight_rows, weight_width), bf16)
    block0, block2, block3, resid_rows, slot_keys, pack, message, w_here = call(
        functools.partial(pack_kernel, capacity),
        [
            block, ((block_rows + asked_rows, padded), bf16), block,
            ((masked, width), bf16), ((4, 2 * masked), jnp.int32), shard,
            ((message_rows, width), bf16),
            ((quarter + masked // 2, width), bf16),
        ],
        [
            ((block_rows, width), bf16), ((4, block_rows, padded), bf16), ((tokens, width), bf16),
            ((tokens, width), bf16), (mask_list.shape, jnp.int32), (owners.shape, jnp.int32),
        ],
        t_query[0], t_key[0], t_value[0], t_resid[0], mask_list, owners,
        w_query, w_key, w_value, w_out, w_proj, pred_query[0], pred_context[0], w_out_teacher,
        far=14, copies=17,
    )
    other2, other3, w_cam = send(block2, 2), send(block3, 3), send(w_here, 4)
    peer_message = send(message, 1)
    held, passed = call(
        functools.partial(hold_kernel, quarter + masked // 2 + masked),
        [((2 * weight_rows, weight_width), bf16), ((asked_rows, pred_width), bf16)],
        [],
        pack, other2, peer_message,
    )
    first = send_by_core(held, 2, 4)
    far = send(passed, 4)
    slots = ((16 * capacity, padded), bf16)
    own_slots, away_slots, w_pass = call(
        functools.partial(teacher_kernel, capacity, head_size, tokens, masked),
        [slots, slots, (w_out_teacher.shape, bf16)],
        [
            ((4 * masked, padded), bf16), ((4 * tokens, padded), bf16), ((4 * tokens, padded), bf16),
            ((4 * masked, padded), bf16),
        ],
        slot_keys, block0, peer_message, other2, other3, w_cam,
    )
    peer_slots, w_both = send(away_slots, 1), send(w_pass, 1)
    part = ((4 * capacity, width), bf16)
    part0, part1, part2, part3 = call(
        functools.partial(project_kernel, capacity),
        [part] * 4,
        [((2 * padded, width), bf16), ((2 * masked, width), bf16), ((4 * capacity, width), f32)],
        slot_keys, own_slots, peer_slots, w_here, w_cam, peer_message, w_both, resid_rows,
    )
    far1, far2, far3 = send(part1, 2), send(part2, 4), send(part3, 6)
    bundle, forward = call(
        bundle_kernel,
        [((2 * weight_rows, weight_width + 4 * pred_width), bf16), shard],
        [],
        first, other2, far, w_cam, part0,
        after=1,
    )
    peers, third = send(bundle, 1), send_by_core(forward, 4, 2)
    left, right = call(
        split_kernel,
        [((weight_rows, 4 * pred_width), bf16), ((weight_rows, width), bf16)],
        [],
        third, peers,
        after=1,
    )
    (predicted,) = call(
        functools.partial(predict_kernel, capacity, quarter),
        [((8 * capacity, width), f32)],
        [
            ((8 * capacity, pred_width), bf16), ((8 * weight_rows, weight_width), bf16),
            ((8 * context_rows, pred_width), bf16), ((8 * masked, pred_width), bf16),
        ],
        slot_keys, w_here, peer_message, w_cam, other2, far,
        held, first, third, send(left, 1), send(right, 1), peers,
    )
    (errors,) = call(
        functools.partial(finish_kernel, capacity, masked),
        [((8 * capacity, width), bf16)],
        [],
        owners, predicted, part0, far1, far2, far3,
    )
    return errors[None, None]


def solution(mesh):
    placed = (
        P(("clip", "cam"), "slab", None),
        P(("clip", "cam"), "slab", None),
        P(("clip", "cam"), "slab", None),
        P(("clip", "cam"), "slab", None),
        P(("cam", "slab"), None),
        P(("clip", "cam"), "slab", None),
        P(("clip", "cam"), "slab", None),
        P(("cam", "slab"), None),
        P(("cam", "slab"), None),
        P(("cam", "slab"), None),
        P(("cam", "slab"), None),
        P(("cam", "slab"), None),
        P(("clip", "cam"), "slab"),
        P("clip", None),
    )
    small = (mesh.shape["cam"], mesh.shape["slab"]) == (2, 4) and mesh.shape["clip"] % 2 == 0
    return jax.shard_map(
        paired_shards if small else shards,
        mesh=mesh,
        in_specs=placed,
        out_specs=P(("clip", "cam"), "slab", None, None),
        check_vma=False,
    )
```

```python
import functools
import math

import jax
import jax.numpy as jnp
from jax import lax
from jax.experimental import pallas as pl
from jax.experimental.pallas import tpu as pltpu
from jax.sharding import PartitionSpec as P

HEADS = 16
P_HEADS = 12
LANES = 128


def norm_rows(values_in):
    average = jnp.mean(values_in, axis=-1, keepdims=True)
    centered = values_in - average
    variance = jnp.mean(centered * centered, axis=-1, keepdims=True)
    return centered * lax.rsqrt(variance + 1e-06)


def empty_state(row_count, head_count, head_size):
    return (
        jnp.full((row_count, head_count), -1e30, jnp.float32),
        jnp.zeros((row_count, head_count), jnp.float32),
        jnp.zeros((row_count, head_count, head_size), jnp.float32),
    )


def attend_block(state_now, query_heads, key_rows, value_rows):
    head_count = query_heads.shape[1]
    head_size = query_heads.shape[2]
    running_max, weight_sum, accumulated = state_now
    for offset in range(0, key_rows.shape[0], 512):
        key_block = key_rows[offset : offset + 512].reshape(-1, head_count, head_size)
        value_block = value_rows[offset : offset + 512].reshape(-1, head_count, head_size)
        scores = jnp.einsum(
            "rhd,khd->rhk", query_heads, key_block, preferred_element_type=jnp.float32
        ) / math.sqrt(head_size)
        new_max = jnp.maximum(running_max, jnp.max(scores, axis=2))
        rescale = jnp.exp(running_max - new_max)
        exponent = jnp.exp(scores - new_max[:, :, None])
        weight_sum = weight_sum * rescale + jnp.sum(exponent, axis=2)
        accumulated = accumulated * rescale[:, :, None] + jnp.einsum(
            "rhk,khd->rhd",
            exponent.astype(jnp.bfloat16),
            value_block,
            preferred_element_type=jnp.float32,
        )
        running_max = new_max
    return (running_max, weight_sum, accumulated)


def finish_heads(weight_sum, accumulated):
    mixed = accumulated / weight_sum[:, :, None]
    return mixed.reshape(mixed.shape[0], -1).astype(jnp.bfloat16)


def shards(
    t_query,
    t_key,
    t_value,
    t_resid,
    w_out_teacher,
    pred_query,
    pred_context,
    w_query,
    w_key,
    w_value,
    w_out,
    w_proj,
    mask_list,
    owners,
):
    model_width = t_query.shape[2]
    head_size = model_width // HEADS
    local_rows = mask_list[0]
    masked_count = local_rows.shape[0]
    masked_query = jnp.take(t_query[0], local_rows, axis=0)
    masked_resid = jnp.take(t_resid[0], local_rows, axis=0)
    query_heads = masked_query.reshape(masked_count, HEADS, head_size)
    pieces = (
        lax.all_gather(t_key[0], "slab", axis=0, tiled=True),
        lax.all_gather(t_value[0], "slab", axis=0, tiled=True),
    )
    running_max, weight_sum, accumulated = attend_block(
        empty_state(masked_count, HEADS, head_size), query_heads, pieces[0], pieces[1]
    )
    teacher_attended = finish_heads(weight_sum, accumulated)
    projected = jnp.dot(
        teacher_attended,
        lax.all_gather(w_out_teacher, ("cam", "slab"), axis=0, tiled=True),
        preferred_element_type=jnp.float32,
    )
    targets = norm_rows(masked_resid.astype(jnp.float32) + projected).astype(jnp.bfloat16)
    devices = lax.axis_size(("cam", "slab"))
    capacity = 2 * masked_count // devices
    myself = lax.axis_index(("cam", "slab"))
    own_dest = lax.dynamic_index_in_dim(
        owners.reshape(devices, masked_count), myself, 0, keepdims=False
    )
    earlier = jnp.tril(jnp.ones((masked_count, masked_count), jnp.bool_), -1)
    same_owner = own_dest[:, None] == own_dest[None, :]
    order_rank = jnp.sum((same_owner & earlier).astype(jnp.int32), axis=1)
    slot_index = own_dest * capacity + order_rank
    slot_total = devices * capacity
    query_rows = pred_query[0]
    pred_width = query_rows.shape[1]
    full_query, full_key, full_value, full_out, full_proj = (
        lax.all_gather(w_query, ("cam", "slab"), axis=0, tiled=True),
        lax.all_gather(w_key, ("cam", "slab"), axis=0, tiled=True),
        lax.all_gather(w_value, ("cam", "slab"), axis=0, tiled=True),
        lax.all_gather(w_out, ("cam", "slab"), axis=0, tiled=True),
        lax.all_gather(w_proj, ("cam", "slab"), axis=0, tiled=True),
    )
    pred_head = pred_width // P_HEADS
    pred_heads = (
        jnp.dot(query_rows, full_query, preferred_element_type=jnp.float32)
        .astype(jnp.bfloat16)
        .reshape(masked_count, P_HEADS, pred_head)
    )
    start_state = empty_state(masked_count, P_HEADS, pred_head)
    context = lax.all_gather(pred_context[0], ("cam", "slab"), axis=0, tiled=True)
    context_keys = jnp.dot(context, full_key, preferred_element_type=jnp.float32)
    context_values = jnp.dot(context, full_value, preferred_element_type=jnp.float32)
    running_max, weight_sum, accumulated = attend_block(
        start_state,
        pred_heads,
        context_keys.astype(jnp.bfloat16),
        context_values.astype(jnp.bfloat16),
    )
    pred_attended = finish_heads(weight_sum, accumulated)
    pred_hidden = query_rows.astype(jnp.float32) + jnp.dot(
        pred_attended, full_out, preferred_element_type=jnp.float32
    )
    predicted = norm_rows(pred_hidden).astype(jnp.bfloat16)
    difference = jnp.dot(
        predicted, full_proj, preferred_element_type=jnp.float32
    ) - targets.astype(jnp.float32)
    sent = (
        jnp.zeros((slot_total, model_width), jnp.bfloat16)
        .at[slot_index]
        .set(difference.astype(jnp.bfloat16))
        .reshape(devices, capacity, model_width)
    )
    errors = lax.all_to_all(sent, ("cam", "slab"), split_axis=0, concat_axis=0, tiled=True)
    return errors.reshape(1, 1, slot_total, model_width)


def rows_dot(left, right):
    return lax.dot_general(
        left, right, (((1,), (1,)), ((), ())), preferred_element_type=jnp.float32
    )


def dot(left, right):
    return jnp.dot(left, right, preferred_element_type=jnp.float32)


def position():
    return lax.axis_index("cam"), lax.axis_index("slab")


def head_windows(head_count, head_size):
    windows = []
    for head in range(head_count):
        low, high = head * head_size, (head + 1) * head_size
        start = low // LANES * LANES
        windows.append((low, high, start, -(-high // LANES) * LANES))
    return windows


def inside(shape, start, low, high):
    lane = lax.broadcasted_iota(jnp.int32, shape, 1) + start
    return (lane >= low) & (lane < high)


def softmax_terms(scores, scale):
    peak = jnp.max(scores, axis=1, keepdims=True)
    terms = jnp.exp2((scores - peak) * scale)
    return terms.astype(jnp.bfloat16), jnp.sum(terms, axis=1, keepdims=True)


def slot_picker(key_row, owner, capacity, slot_total):
    shape = (2 * capacity, key_row.shape[1])
    row = lax.broadcasted_iota(jnp.int32, shape, 0)
    late = row >= capacity
    wanted = owner * capacity + row + jnp.where(late, slot_total - capacity, 0)
    return jnp.where(key_row == wanted, 1.0, 0.0).astype(jnp.bfloat16)


def pack_kernel(
    capacity, query, key, value, resid, mask, owners, wq, wk, wv, wo, wp, asks, context, w_far,
    block0, block2, block3, resid_rows, slot_keys, pack, message, w_here,
    stack, blocks, query_here, resid_here, mask_here, owners_here, done,
):
    cam, slab = position()
    tokens, width = key.shape
    masked, pred_width = asks.shape
    quarter = width // 8
    context_rows = context.shape[0]
    row_total = stack.shape[0]
    half = masked // 2
    moves = [
        (mask, mask_here),
        (owners, owners_here),
        (query, query_here),
        (key, stack.at[0:tokens]),
        (value, stack.at[tokens : 2 * tokens]),
        (resid, resid_here),
        (w_far, w_here),
    ]
    at = 0
    for part in (wq, wk, wv, wo, wp):
        moves.append((part, pack.at[:, at : at + part.shape[1]]))
        at += part.shape[1]
    moves.append((asks.at[0:half], pack.at[:, at : at + pred_width]))
    moves.append((asks.at[half:], pack.at[:, at + pred_width : at + 2 * pred_width]))
    at += 2 * pred_width
    split, rest = pack.shape[1] - at, half - context_rows
    moves.append((context.at[:, 0:split], pack.at[0:context_rows, at:]))
    for number in range(context_rows // rest):
        lanes = slice(at + number * (pred_width - split), at + (number + 1) * (pred_width - split))
        moves.append(
            (
                context.at[number * rest : (number + 1) * rest, split:],
                pack.at[context_rows:, lanes],
            )
        )
    copies = [
        pltpu.make_async_copy(source, target, done.at[number])
        for number, (source, target) in enumerate(moves)
    ]
    for copy in copies:
        copy.start()
    token = lax.broadcasted_iota(jnp.int32, (tokens, masked), 0)
    copies[0].wait()
    chosen = jnp.where(token == mask_here[...], 1.0, 0.0).T.astype(jnp.bfloat16)
    copies[1].wait()
    listed = owners.shape[1]
    before = lax.broadcasted_iota(jnp.int32, (listed, listed), 0)
    after = lax.broadcasted_iota(jnp.int32, (listed, listed), 1)
    group = sum((before >= edge).astype(jnp.int32) for edge in range(masked, listed, masked))
    group_after = sum((after >= edge).astype(jnp.int32) for edge in range(masked, listed, masked))
    precedes = jnp.where((before < after) & (group == group_after), 1.0, 0.0)
    precedes = precedes.astype(jnp.bfloat16)
    lane = lax.broadcasted_iota(jnp.int32, (1, listed), 1)
    odd = ((lane >= masked) & (lane < 2 * masked)) | (lane >= 3 * masked)
    device = lax.broadcasted_iota(jnp.int32, (8, listed), 0)
    for camera in range(2):
        owner_row = owners_here[camera : camera + 1, :]
        owned = jnp.where(device == owner_row, 1.0, 0.0)
        counted = dot(owned.astype(jnp.bfloat16), precedes)
        rank = jnp.sum(owned * counted, axis=0, keepdims=True).astype(jnp.int32)
        keys = owner_row * capacity + rank + jnp.where(odd, 8 * capacity, 0)
        slot_keys[2 * camera : 2 * camera + 1, :] = keys[:, 0 : 2 * masked]
        slot_keys[2 * camera + 1 : 2 * camera + 2, :] = keys[:, 2 * masked :]
    for copy in copies[2:5]:
        copy.wait()
    stack[2 * tokens :] = dot(chosen, query_here[...]).astype(jnp.bfloat16)
    pad = blocks.shape[2] - 2 * quarter
    for other in range(4):
        first = stack[:, other * quarter : (other + 1) * quarter]
        second = stack[:, (other + 4) * quarter : (other + 5) * quarter]
        blocks[other] = jnp.concatenate(
            [first, second, jnp.zeros((row_total, pad), jnp.bfloat16)], axis=1
        )
    for relation, out in ((0, block0), (2, block2), (3, block3)):
        out[0:row_total] = blocks[slab ^ relation]
    core_block = blocks.at[slab ^ 1]
    for copy in copies[5:]:
        copy.wait()
    resid_rows[...] = dot(chosen, resid_here[...]).astype(jnp.bfloat16)
    base = w_here.shape[0]
    message[0:base] = w_here[...]
    message[base : base + masked] = resid_rows[...]
    base += masked
    count = pack.shape[0]
    total = pack.shape[1]
    message[base + 2 * count : base + 3 * count] = jnp.zeros((count, width), jnp.bfloat16)
    for low in range(0, total, width):
        high = min(low + width, total)
        message[base : base + count, 0 : high - low] = pack[:, low:high]
        base += count
    message[base:] = jnp.zeros((tokens, width), jnp.bfloat16)
    for number in range(3):
        low, high = number * tokens, min((number + 1) * tokens, row_total)
        lanes = slice(number * core_block.shape[1], (number + 1) * core_block.shape[1])
        message[base : base + high - low, lanes] = core_block[low:high]


def hold_kernel(base, pack, message, after, held):
    core = lax.axis_index("slab") % 2
    rows, wide = pack.shape
    width = message.shape[1]
    held[pl.ds(pl.multiple_of(core * rows, rows), rows)] = pack[...]
    other = pl.ds(pl.multiple_of((1 - core) * rows, rows), rows)
    for number, low in enumerate(range(0, wide, width)):
        high = min(low + width, wide)
        at = base + number * rows
        held[other, low:high] = message[at : at + rows, 0 : high - low]


def bundle_kernel(first, after, out, forward):
    core = lax.axis_index("slab") % 2
    part = forward.shape[0]
    forward[...] = first[pl.ds(pl.multiple_of(core * part, part), part)]
    out[...] = first[...]


def split_kernel(piece, after, left, right):
    left[...] = piece[:, 0 : left.shape[1]]
    right[...] = piece[:, left.shape[1] :]


def teacher_kernel(
    capacity, head_size, tokens, masked, slot_keys, block0, message, block2, block3,
    own_core, peer_core, queries, keys, values, attended,
):
    cam, slab = position()
    wide, base = keys.shape[1], message.shape[0] - tokens
    pieces = [message.at[base:, number * wide : (number + 1) * wide] for number in range(3)]
    for relation, block in enumerate((block0, None, block2, block3)):
        if relation == 1:
            key_part, value_part, query_part = pieces
            query_part = query_part.at[0:masked]
        else:
            key_part, value_part = block.at[0:tokens], block.at[tokens : 2 * tokens]
            query_part = block.at[2 * tokens : 2 * tokens + masked]
        keys[relation * tokens : (relation + 1) * tokens] = key_part[...]
        values[relation * tokens : (relation + 1) * tokens] = value_part[...]
        start = pl.multiple_of((slab ^ relation) * masked, masked)
        queries[pl.ds(start, masked)] = query_part[...]
    scale = math.log2(math.e) / math.sqrt(head_size)
    chunk = 2 * masked
    for half in range(2):
        rows = slice(half * chunk, (half + 1) * chunk)
        total = [jnp.zeros((chunk, LANES), jnp.float32) for _ in range(attended.shape[1] // LANES)]
        for low, high, start, stop in head_windows(4, head_size):
            window = inside((chunk, stop - start), start, low, high)
            picked = jnp.where(window, queries[rows, start:stop].astype(jnp.float32), 0.0)
            scores = rows_dot(picked.astype(jnp.bfloat16), keys[:, start:stop])
            terms, weight = softmax_terms(scores, scale)
            mixed = dot(terms, values[:, start:stop]) / weight
            mixed = jnp.where(window, mixed, 0.0)
            for tile in range(start // LANES, stop // LANES):
                total[tile] += mixed[:, tile * LANES - start : (tile + 1) * LANES - start]
        attended[rows] = jnp.concatenate(total, axis=1).astype(jnp.bfloat16)
    for flip, out in enumerate((own_core, peer_core)):
        for relation in range(4):
            owner = (cam * 4 + slab) ^ (relation * 2 + flip)
            for half in range(2):
                picker = slot_picker(slot_keys[pl.ds(2 * cam + half, 1), :], owner, capacity, 8 * capacity)
                at = (relation * 2 + half) * 2 * capacity
                out[at : at + 2 * capacity] = dot(
                    picker, attended[half * chunk : (half + 1) * chunk]
                ).astype(jnp.bfloat16)


def pass_kernel(rows, after, out):
    out[...] = rows[...]


def project_kernel(
    capacity, slot_keys, own_slots, peer_slots, w_own, w_cam, w_core, w_both, resid_own,
    out0, out1, out2, out3, weight, resid_pair, total,
):
    cam, slab = position()
    core, chip = slab % 2, slab // 2
    width = w_own.shape[1]
    part = width // 8
    half = own_slots.shape[1]
    for base, same, crossed in ((0, w_own, w_cam), (half, w_core, w_both)):
        weight[pl.ds(pl.multiple_of(base + cam * part, 16), part)] = same[0:part]
        weight[pl.ds(pl.multiple_of(base + (1 - cam) * part, 16), part)] = crossed[0:part]
        weight[base + 2 * part : base + half] = jnp.zeros((half - 2 * part, width), jnp.bfloat16)
    rows = resid_own.shape[0]
    resid_pair[pl.ds(pl.multiple_of(core * rows, rows), rows)] = resid_own[...]
    resid_pair[pl.ds(pl.multiple_of((1 - core) * rows, rows), rows)] = w_core[
        w_own.shape[0] : w_own.shape[0] + rows
    ]
    key_row = slot_keys[pl.ds(2 * cam + chip, 1), :]
    block = out0.shape[0]
    for relation, out in ((3, out3), (2, out2), (1, out1), (0, out0)):
        at = relation * block
        total[...] = dot(own_slots[at : at + block], weight[0:half]) + dot(
            peer_slots[at : at + block], weight[half:]
        )
        owner = (cam * 4 + slab) ^ (relation * 2)
        picker = slot_picker(key_row, owner, capacity, 8 * capacity)
        own_rows = pl.ds(pl.multiple_of(chip * 2 * capacity, 8), 2 * capacity)
        total[own_rows] = total[own_rows] + dot(picker, resid_pair[...])
        out[...] = total[...].astype(jnp.bfloat16)


def predict_kernel(
    capacity, base, slot_keys, message, own_pack, first, third, peer_left, peer_right, peers, out,
    queries, weights, context, asks, peer_pack,
):
    cam, slab = position()
    core = slab % 2
    own = cam * 4 + slab
    part, total = third.shape
    wide = weights.shape[1]
    width = context.shape[1]
    context_rows = context.shape[0] // 8
    masked = asks.shape[0] // 8

    def place(source, piece):
        weights[pl.ds(pl.multiple_of(source * part, part), part)] = piece[:, 0:wide]
        for number in range(2):
            start = pl.multiple_of(source * masked + number * part, part)
            low = wide + number * width
            asks[pl.ds(start, part)] = piece[:, low : low + width]
        low = wide + 2 * width
        split, rest = total - low, part - context_rows
        start = pl.multiple_of(source * context_rows, context_rows)
        context[pl.ds(start, context_rows), 0:split] = piece[0:context_rows, low:]
        for number in range(context_rows // rest):
            at = low + number * (width - split)
            context[pl.ds(pl.multiple_of(start + number * rest, rest), rest), split:] = piece[
                context_rows:, at : at + width - split
            ]

    place(own, own_pack)
    for number, low in enumerate(range(0, total, message.shape[1])):
        high = min(low + message.shape[1], total)
        at = base + number * part
        peer_pack[:, low:high] = message[at : at + part, 0 : high - low]
    place(own ^ 1, peer_pack)
    chip = own - core
    along, across = jnp.where(core == 0, 2, 4), jnp.where(core == 0, 4, 2)
    for flip in range(2):
        place((chip ^ along) + flip, first.at[flip * part : (flip + 1) * part])
        place((chip ^ across) + flip, peers.at[flip * part : (flip + 1) * part])
    place(own ^ 6, third)
    peer_pack[:, 0 : peer_left.shape[1]] = peer_left[...]
    peer_pack[:, peer_left.shape[1] :] = peer_right[...]
    place(own ^ 7, peer_pack)
    for chip in range(4):
        picker = slot_picker(slot_keys[chip : chip + 1, :], own, capacity, 8 * capacity)
        queries[chip * 2 * capacity : (chip + 1) * 2 * capacity] = dot(
            picker, asks[chip * 2 * masked : (chip + 1) * 2 * masked]
        ).astype(jnp.bfloat16)
    head_size = width // P_HEADS
    scale = math.log2(math.e) / math.sqrt(head_size)
    asked = dot(queries[...], weights[:, 0:width]).astype(jnp.bfloat16)
    seen_keys = dot(context[...], weights[:, width : 2 * width]).astype(jnp.bfloat16)
    seen_values = dot(context[...], weights[:, 2 * width : 3 * width]).astype(jnp.bfloat16)
    total = [jnp.zeros((asked.shape[0], LANES), jnp.float32) for _ in range(width // LANES)]
    for low, high, start, stop in head_windows(P_HEADS, head_size):
        window = inside((asked.shape[0], stop - start), start, low, high)
        picked = jnp.where(window, asked[:, start:stop].astype(jnp.float32), 0.0)
        scores = rows_dot(picked.astype(jnp.bfloat16), seen_keys[:, start:stop])
        terms, weight = softmax_terms(scores, scale)
        mixed = dot(terms, seen_values[:, start:stop]) / weight
        total[start // LANES] += jnp.where(window, mixed, 0.0)
    attended = jnp.concatenate(total, axis=1).astype(jnp.bfloat16)
    hidden = queries[...].astype(jnp.float32) + dot(attended, weights[:, 3 * width : 4 * width])
    predicted = norm_rows(hidden).astype(jnp.bfloat16)
    out[...] = dot(predicted, weights[:, 4 * width :])


def error_rows(capacity, masked, owner, listed, predicted, near, far):
    rows = near.shape[0]
    summed = near[...].astype(jnp.float32) + far[...].astype(jnp.float32)
    shape = (rows, listed.shape[1])
    row = lax.broadcasted_iota(jnp.int32, shape, 0)
    lane = lax.broadcasted_iota(jnp.int32, shape, 1)
    same = jnp.zeros(shape, jnp.bool_)
    for group in range(4):
        same = same | (
            (row >= group * capacity)
            & (row < (group + 1) * capacity)
            & (lane >= group * masked)
            & (lane < (group + 1) * masked)
        )
    count = jnp.sum(jnp.where(same & (listed == owner), 1.0, 0.0), axis=1, keepdims=True)
    order = lax.broadcasted_iota(jnp.int32, (rows, 1), 0)
    order = order - sum(
        jnp.where(order >= group * capacity, capacity, 0) for group in range(1, 4)
    )
    filled = order.astype(jnp.float32) < count
    goal = norm_rows(summed).astype(jnp.bfloat16).astype(jnp.float32)
    return jnp.where(filled, predicted - goal, 0.0).astype(jnp.bfloat16)


def own_camera_kernel(capacity, masked, owners, predicted, near, far, out):
    cam, slab = position()
    rows = near.shape[0]
    at = pl.ds(pl.multiple_of(cam * rows, rows), rows)
    listed = owners[pl.ds(cam, 1), :]
    out[...] = error_rows(capacity, masked, cam * 4 + slab, listed, predicted[at], near, far)


def other_camera_kernel(
    capacity, masked, owners, predicted, first_rows, near, far, out, here, done
):
    cam, slab = position()
    rows = near.shape[0]
    own = pl.ds(pl.multiple_of(cam * rows, rows), rows)
    at = pl.ds(pl.multiple_of((1 - cam) * rows, rows), rows)
    early = pltpu.make_async_copy(first_rows, out.at[own], done.at[0])
    early.start()
    listed = owners[pl.ds(1 - cam, 1), :]
    here[...] = error_rows(capacity, masked, cam * 4 + slab, listed, predicted[at], near, far)
    late = pltpu.make_async_copy(here, out.at[at], done.at[1])
    late.start()
    early.wait()
    late.wait()


def call(kernel, outs, scratch, *args, far=0, copies=0, after=0, out_space=pltpu.VMEM):
    shapes = tuple(jax.ShapeDtypeStruct(shape, dtype) for shape, dtype in outs)
    near = pl.BlockSpec(memory_space=pltpu.VMEM)
    scratch_shapes = [pltpu.VMEM(shape, dtype) for shape, dtype in scratch]
    if copies:
        scratch_shapes.append(pltpu.SemaphoreType.DMA((copies,)))
    if far:
        args = [pltpu.with_memory_space_constraint(arg, pltpu.HBM) for arg in args[:far]] + list(args[far:])
    return pl.pallas_call(
        kernel,
        out_shape=shapes,
        in_specs=[pl.BlockSpec(memory_space=pltpu.HBM)] * far
        + [near] * (len(args) - far - after)
        + [pl.BlockSpec(memory_space=pl.ANY)] * after,
        out_specs=tuple(pl.BlockSpec(memory_space=out_space) for _ in outs),
        scratch_shapes=scratch_shapes,
        compiler_params=pltpu.CompilerParams(vmem_limit_bytes=40 * 2**20),
    )(*args)


def send(rows, flip):
    return lax.ppermute(rows, ("cam", "slab"), [(source, source ^ flip) for source in range(8)])


def send_by_core(rows, even, odd):
    pairs = [(source, source ^ (odd if source % 2 else even)) for source in range(8)]
    return lax.ppermute(rows, ("cam", "slab"), pairs)


def paired_shards(
    t_query, t_key, t_value, t_resid, w_out_teacher, pred_query, pred_context,
    w_query, w_key, w_value, w_out, w_proj, mask_list, owners,
):
    bf16, f32 = jnp.bfloat16, jnp.float32
    tokens, width = t_key.shape[1:]
    masked, pred_width = pred_query.shape[1:]
    capacity = masked // 4
    quarter = width // 8
    head_size = width // HEADS
    context_rows = pred_context.shape[1]
    padded = -(-2 * quarter // LANES) * LANES
    block_rows = 2 * tokens + masked
    block = ((block_rows, padded), bf16)
    weight_rows = w_query.shape[0]
    weight_width = 4 * pred_width + w_proj.shape[1]
    pack_width = weight_width + 2 * pred_width + context_rows * pred_width // weight_rows
    pack_at = quarter + masked
    message_rows = pack_at - pack_width // -width * weight_rows + tokens
    shard = ((weight_rows, pack_width), bf16)
    block0, block2, block3, resid_rows, slot_keys, pack, message, w_here = call(
        functools.partial(pack_kernel, capacity),
        [
            block, block, block, ((masked, width), bf16), ((4, 2 * masked), jnp.int32), shard,
            ((message_rows, width), bf16), ((quarter, width), bf16),
        ],
        [
            ((block_rows, width), bf16), ((4, block_rows, padded), bf16), ((tokens, width), bf16),
            ((tokens, width), bf16), (mask_list.shape, jnp.int32), (owners.shape, jnp.int32),
        ],
        t_query[0], t_key[0], t_value[0], t_resid[0], mask_list, owners,
        w_query, w_key, w_value, w_out, w_proj, pred_query[0], pred_context[0], w_out_teacher,
        far=14, copies=17,
    )
    other2, other3 = send(block2, 2), send(block3, 3)
    w_cam = send(w_here, 4)
    peer_message = send(message, 1)
    pair = ((2 * weight_rows, pack_width), bf16)
    (held,) = call(
        functools.partial(hold_kernel, pack_at), [pair], [], pack, peer_message, other2, after=1
    )
    first = send_by_core(held, 2, 4)
    slots = ((16 * capacity, padded), bf16)
    own_slots, away_slots = call(
        functools.partial(teacher_kernel, capacity, head_size, tokens, masked),
        [slots, slots],
        [
            ((4 * masked, padded), bf16), ((4 * tokens, padded), bf16), ((4 * tokens, padded), bf16),
            ((4 * masked, padded), bf16),
        ],
        slot_keys, block0, peer_message, other2, other3,
    )
    peer_slots = send(away_slots, 1)
    (w_pass,) = call(pass_kernel, [((quarter, width), bf16)], [], w_cam, own_slots, after=1)
    w_both = send(w_pass, 1)
    part = ((4 * capacity, width), bf16)
    part0, part1, part2, part3 = call(
        functools.partial(project_kernel, capacity),
        [part] * 4,
        [((2 * padded, width), bf16), ((2 * masked, width), bf16), ((4 * capacity, width), f32)],
        slot_keys, own_slots, peer_slots, w_here, w_cam, peer_message,
        w_both, resid_rows,
    )
    far1, far2, far3 = send(part1, 2), send(part2, 4), send(part3, 6)
    bundle, forward = call(bundle_kernel, [pair, shard], [], first, part0, after=1)
    peers, third = send(bundle, 1), send_by_core(forward, 4, 2)
    left_width = pack_width // 2 // LANES * LANES
    halves = [((weight_rows, lanes), bf16) for lanes in (left_width, pack_width - left_width)]
    left, right = call(
        split_kernel, halves, [], third, peers, after=1
    )
    (predicted,) = call(
        functools.partial(predict_kernel, capacity, pack_at),
        [((8 * capacity, width), f32)],
        [
            ((8 * capacity, pred_width), bf16), ((8 * weight_rows, weight_width), bf16),
            ((8 * context_rows, pred_width), bf16), ((8 * masked, pred_width), bf16), shard,
        ],
        slot_keys, peer_message, pack, first, third, send(left, 1), send(right, 1), peers,
    )
    (first_rows,) = call(
        functools.partial(own_camera_kernel, capacity, masked),
        [part],
        [],
        owners, predicted, part0, far1,
    )
    (errors,) = call(
        functools.partial(other_camera_kernel, capacity, masked),
        [((8 * capacity, width), bf16)],
        [part],
        owners, predicted, first_rows, far2, far3,
        copies=2, out_space=pltpu.HBM,
    )
    return errors[None, None]


def solution(mesh):
    placed = (
        P(("clip", "cam"), "slab", None),
        P(("clip", "cam"), "slab", None),
        P(("clip", "cam"), "slab", None),
        P(("clip", "cam"), "slab", None),
        P(("cam", "slab"), None),
        P(("clip", "cam"), "slab", None),
        P(("clip", "cam"), "slab", None),
        P(("cam", "slab"), None),
        P(("cam", "slab"), None),
        P(("cam", "slab"), None),
        P(("cam", "slab"), None),
        P(("cam", "slab"), None),
        P(("clip", "cam"), "slab"),
        P("clip", None),
    )
    small = (mesh.shape["cam"], mesh.shape["slab"]) == (2, 4) and mesh.shape["clip"] % 2 == 0
    return jax.shard_map(
        paired_shards if small else shards,
        mesh=mesh,
        in_specs=placed,
        out_specs=P(("clip", "cam"), "slab", None, None),
        check_vma=False,
    )
```

```python
import functools
import math

import jax
import jax.numpy as jnp
from jax import lax
from jax.experimental import pallas as pl
from jax.experimental.pallas import tpu as pltpu
from jax.sharding import PartitionSpec as P

HEADS = 16
P_HEADS = 12
LANES = 128


def norm_rows(values_in):
    average = jnp.mean(values_in, axis=-1, keepdims=True)
    centered = values_in - average
    variance = jnp.mean(centered * centered, axis=-1, keepdims=True)
    return centered * lax.rsqrt(variance + 1e-06)


def empty_state(row_count, head_count, head_size):
    return (
        jnp.full((row_count, head_count), -1e30, jnp.float32),
        jnp.zeros((row_count, head_count), jnp.float32),
        jnp.zeros((row_count, head_count, head_size), jnp.float32),
    )


def attend_block(state_now, query_heads, key_rows, value_rows):
    head_count = query_heads.shape[1]
    head_size = query_heads.shape[2]
    running_max, weight_sum, accumulated = state_now
    for offset in range(0, key_rows.shape[0], 512):
        key_block = key_rows[offset : offset + 512].reshape(-1, head_count, head_size)
        value_block = value_rows[offset : offset + 512].reshape(-1, head_count, head_size)
        scores = jnp.einsum(
            "rhd,khd->rhk", query_heads, key_block, preferred_element_type=jnp.float32
        ) / math.sqrt(head_size)
        new_max = jnp.maximum(running_max, jnp.max(scores, axis=2))
        rescale = jnp.exp(running_max - new_max)
        exponent = jnp.exp(scores - new_max[:, :, None])
        weight_sum = weight_sum * rescale + jnp.sum(exponent, axis=2)
        accumulated = accumulated * rescale[:, :, None] + jnp.einsum(
            "rhk,khd->rhd",
            exponent.astype(jnp.bfloat16),
            value_block,
            preferred_element_type=jnp.float32,
        )
        running_max = new_max
    return (running_max, weight_sum, accumulated)


def finish_heads(weight_sum, accumulated):
    mixed = accumulated / weight_sum[:, :, None]
    return mixed.reshape(mixed.shape[0], -1).astype(jnp.bfloat16)


def shards(
    t_query,
    t_key,
    t_value,
    t_resid,
    w_out_teacher,
    pred_query,
    pred_context,
    w_query,
    w_key,
    w_value,
    w_out,
    w_proj,
    mask_list,
    owners,
):
    model_width = t_query.shape[2]
    head_size = model_width // HEADS
    local_rows = mask_list[0]
    masked_count = local_rows.shape[0]
    masked_query = jnp.take(t_query[0], local_rows, axis=0)
    masked_resid = jnp.take(t_resid[0], local_rows, axis=0)
    query_heads = masked_query.reshape(masked_count, HEADS, head_size)
    pieces = (
        lax.all_gather(t_key[0], "slab", axis=0, tiled=True),
        lax.all_gather(t_value[0], "slab", axis=0, tiled=True),
    )
    running_max, weight_sum, accumulated = attend_block(
        empty_state(masked_count, HEADS, head_size), query_heads, pieces[0], pieces[1]
    )
    teacher_attended = finish_heads(weight_sum, accumulated)
    projected = jnp.dot(
        teacher_attended,
        lax.all_gather(w_out_teacher, ("cam", "slab"), axis=0, tiled=True),
        preferred_element_type=jnp.float32,
    )
    targets = norm_rows(masked_resid.astype(jnp.float32) + projected).astype(jnp.bfloat16)
    devices = lax.axis_size(("cam", "slab"))
    capacity = 2 * masked_count // devices
    myself = lax.axis_index(("cam", "slab"))
    own_dest = lax.dynamic_index_in_dim(
        owners.reshape(devices, masked_count), myself, 0, keepdims=False
    )
    earlier = jnp.tril(jnp.ones((masked_count, masked_count), jnp.bool_), -1)
    same_owner = own_dest[:, None] == own_dest[None, :]
    order_rank = jnp.sum((same_owner & earlier).astype(jnp.int32), axis=1)
    slot_index = own_dest * capacity + order_rank
    slot_total = devices * capacity
    query_rows = pred_query[0]
    pred_width = query_rows.shape[1]
    full_query, full_key, full_value, full_out, full_proj = (
        lax.all_gather(w_query, ("cam", "slab"), axis=0, tiled=True),
        lax.all_gather(w_key, ("cam", "slab"), axis=0, tiled=True),
        lax.all_gather(w_value, ("cam", "slab"), axis=0, tiled=True),
        lax.all_gather(w_out, ("cam", "slab"), axis=0, tiled=True),
        lax.all_gather(w_proj, ("cam", "slab"), axis=0, tiled=True),
    )
    pred_head = pred_width // P_HEADS
    pred_heads = (
        jnp.dot(query_rows, full_query, preferred_element_type=jnp.float32)
        .astype(jnp.bfloat16)
        .reshape(masked_count, P_HEADS, pred_head)
    )
    start_state = empty_state(masked_count, P_HEADS, pred_head)
    context = lax.all_gather(pred_context[0], ("cam", "slab"), axis=0, tiled=True)
    context_keys = jnp.dot(context, full_key, preferred_element_type=jnp.float32)
    context_values = jnp.dot(context, full_value, preferred_element_type=jnp.float32)
    running_max, weight_sum, accumulated = attend_block(
        start_state,
        pred_heads,
        context_keys.astype(jnp.bfloat16),
        context_values.astype(jnp.bfloat16),
    )
    pred_attended = finish_heads(weight_sum, accumulated)
    pred_hidden = query_rows.astype(jnp.float32) + jnp.dot(
        pred_attended, full_out, preferred_element_type=jnp.float32
    )
    predicted = norm_rows(pred_hidden).astype(jnp.bfloat16)
    difference = jnp.dot(
        predicted, full_proj, preferred_element_type=jnp.float32
    ) - targets.astype(jnp.float32)
    sent = (
        jnp.zeros((slot_total, model_width), jnp.bfloat16)
        .at[slot_index]
        .set(difference.astype(jnp.bfloat16))
        .reshape(devices, capacity, model_width)
    )
    errors = lax.all_to_all(sent, ("cam", "slab"), split_axis=0, concat_axis=0, tiled=True)
    return errors.reshape(1, 1, slot_total, model_width)


def rows_dot(left, right):
    return lax.dot_general(
        left, right, (((1,), (1,)), ((), ())), preferred_element_type=jnp.float32
    )


def dot(left, right):
    return jnp.dot(left, right, preferred_element_type=jnp.float32)


def position():
    return lax.axis_index("cam"), lax.axis_index("slab")


def head_windows(head_count, head_size):
    windows = []
    for head in range(head_count):
        low, high = head * head_size, (head + 1) * head_size
        start = low // LANES * LANES
        windows.append((low, high, start, -(-high // LANES) * LANES))
    return windows


def inside(shape, start, low, high):
    lane = lax.broadcasted_iota(jnp.int32, shape, 1) + start
    return (lane >= low) & (lane < high)


def softmax_terms(scores, scale):
    peak = jnp.max(scores, axis=1, keepdims=True)
    terms = jnp.exp2((scores - peak) * scale)
    return terms.astype(jnp.bfloat16), jnp.sum(terms, axis=1, keepdims=True)


def slot_picker(key_row, owner, capacity, slot_total):
    shape = (2 * capacity, key_row.shape[1])
    row = lax.broadcasted_iota(jnp.int32, shape, 0)
    late = row >= capacity
    wanted = owner * capacity + row + jnp.where(late, slot_total - capacity, 0)
    return jnp.where(key_row == wanted, 1.0, 0.0).astype(jnp.bfloat16)


def pack_kernel(
    capacity, query, key, value, resid, mask, owners, wq, wk, wv, wo, wp, asks, context, w_far,
    block0, block2, block3, resid_rows, slot_keys, pack, message, w_here,
    stack, blocks, query_here, resid_here, mask_here, owners_here, done,
):
    cam, slab = position()
    tokens, width = key.shape
    masked, pred_width = asks.shape
    quarter = width // 8
    context_rows = context.shape[0]
    row_total = stack.shape[0]
    half = masked // 2
    moves = [
        (mask, mask_here),
        (owners, owners_here),
        (query, query_here),
        (key, stack.at[0:tokens]),
        (value, stack.at[tokens : 2 * tokens]),
        (resid, resid_here),
        (w_far, w_here),
        (w_far, message.at[0:quarter]),
    ]
    at = 0
    for part in (wq, wk, wv, wo, wp):
        moves.append((part, pack.at[:, at : at + part.shape[1]]))
        at += part.shape[1]
    moves.append((asks.at[0:half], pack.at[:, at : at + pred_width]))
    moves.append((asks.at[half:], pack.at[:, at + pred_width : at + 2 * pred_width]))
    at += 2 * pred_width
    split, rest = pack.shape[1] - at, half - context_rows
    moves.append((context.at[:, 0:split], pack.at[0:context_rows, at:]))
    for number in range(context_rows // rest):
        lanes = slice(at + number * (pred_width - split), at + (number + 1) * (pred_width - split))
        moves.append(
            (
                context.at[number * rest : (number + 1) * rest, split:],
                pack.at[context_rows:, lanes],
            )
        )
    copies = [
        pltpu.make_async_copy(source, target, done.at[number])
        for number, (source, target) in enumerate(moves)
    ]
    for copy in copies:
        copy.start()
    token = lax.broadcasted_iota(jnp.int32, (tokens, masked), 0)
    copies[0].wait()
    chosen = jnp.where(token == mask_here[...], 1.0, 0.0).T.astype(jnp.bfloat16)
    copies[1].wait()
    listed = owners.shape[1]
    before = lax.broadcasted_iota(jnp.int32, (listed, listed), 0)
    after = lax.broadcasted_iota(jnp.int32, (listed, listed), 1)
    group = sum((before >= edge).astype(jnp.int32) for edge in range(masked, listed, masked))
    group_after = sum((after >= edge).astype(jnp.int32) for edge in range(masked, listed, masked))
    precedes = jnp.where((before < after) & (group == group_after), 1.0, 0.0)
    precedes = precedes.astype(jnp.bfloat16)
    lane = lax.broadcasted_iota(jnp.int32, (1, listed), 1)
    odd = ((lane >= masked) & (lane < 2 * masked)) | (lane >= 3 * masked)
    device = lax.broadcasted_iota(jnp.int32, (8, listed), 0)
    for camera in range(2):
        owner_row = owners_here[camera : camera + 1, :]
        owned = jnp.where(device == owner_row, 1.0, 0.0)
        counted = dot(owned.astype(jnp.bfloat16), precedes)
        rank = jnp.sum(owned * counted, axis=0, keepdims=True).astype(jnp.int32)
        keys = owner_row * capacity + rank + jnp.where(odd, 8 * capacity, 0)
        slot_keys[2 * camera : 2 * camera + 1, :] = keys[:, 0 : 2 * masked]
        slot_keys[2 * camera + 1 : 2 * camera + 2, :] = keys[:, 2 * masked :]
    for copy in copies[2:5]:
        copy.wait()
    stack[2 * tokens :] = dot(chosen, query_here[...]).astype(jnp.bfloat16)
    pad = blocks.shape[2] - 2 * quarter
    for other in range(4):
        first = stack[:, other * quarter : (other + 1) * quarter]
        second = stack[:, (other + 4) * quarter : (other + 5) * quarter]
        blocks[other] = jnp.concatenate(
            [first, second, jnp.zeros((row_total, pad), jnp.bfloat16)], axis=1
        )
    for relation, out in ((0, block0), (2, block2), (3, block3)):
        out[0:row_total] = blocks[slab ^ relation]
    core_block = blocks.at[slab ^ 1]
    for copy in copies[5:]:
        copy.wait()
    picked = dot(chosen, resid_here[...]).astype(jnp.bfloat16)
    resid_rows[...] = picked
    base = quarter + masked
    message[quarter:base] = picked
    count, total = pack.shape
    for low in range(0, total, width):
        high = min(low + width, total)
        message[base : base + count, 0 : high - low] = pack[:, low:high]
        if high - low < width:
            message[base : base + count, high - low :] = jnp.zeros(
                (count, width - high + low), jnp.bfloat16
            )
        base += count
    wide = core_block.shape[1]
    for number in range(3):
        low, high = number * tokens, min((number + 1) * tokens, row_total)
        lanes = slice(number * wide, (number + 1) * wide)
        message[base : base + high - low, lanes] = core_block[low:high]
    message[base + masked :, 2 * wide : 3 * wide] = jnp.zeros((tokens - masked, wide), jnp.bfloat16)
    message[base:, 3 * wide :] = jnp.zeros((tokens, width - 3 * wide), jnp.bfloat16)


def hold_kernel(
    capacity, base, width, context_rows, slot_keys, pack, message, after, held, own_asks,
    peer, pair,
):
    cam, slab = position()
    core = slab % 2
    chip = cam * 4 + slab - core
    part, total = pack.shape
    lanes = message.shape[1]
    for number, low in enumerate(range(0, total, lanes)):
        high = min(low + lanes, total)
        at = base + number * part
        peer[:, low:high] = message[at : at + part, 0 : high - low]
    wide = total - 2 * width - context_rows * width // part
    low, tail = wide + width, wide + 2 * width
    rest = part - context_rows

    def fill(source, packs):
        held[pl.ds(pl.multiple_of(source * part, part), part), 0:wide] = packs[:, 0:wide]
        for number in range(2):
            start = pl.multiple_of((2 * source + number) * part, part)
            pair[pl.ds(start, part)] = packs[:, wide + number * width : wide + (number + 1) * width]

    fill(core, pack)
    fill(1 - core, peer)
    held[part:, low:] = jnp.zeros((part, held.shape[1] - low), jnp.bfloat16)

    def contexts(first, second):
        split = 2 * LANES
        held[0:context_rows, tail:] = first[0:context_rows, tail : tail + LANES]
        held[part : part + context_rows, tail:] = first[0:context_rows, tail + LANES :]
        held[context_rows:part, tail:] = first[context_rows:, tail : tail + LANES]
        held[part + context_rows :, tail:] = first[context_rows:, tail + LANES :]
        held[part : part + context_rows, low : low + split] = second[0:context_rows, tail:]
        for number in range(2):
            at = part + number * rest
            source = slice(tail + number * LANES, tail + (number + 1) * LANES)
            held[at : at + rest, low + split : tail] = second[context_rows:, source]

    @pl.when(core == 0)
    def _():
        contexts(pack, peer)

    @pl.when(core == 1)
    def _():
        contexts(peer, pack)

    key_row = slot_keys[pl.ds(2 * cam + slab // 2, 1), :]

    def slots(owner):
        picker = slot_picker(key_row, owner, capacity, 8 * capacity)
        return dot(picker, pair[...]).astype(jnp.bfloat16)

    beside = chip ^ jnp.where(core == 0, 2, 4)
    held[0:part, wide:low] = slots(beside)
    held[part:, wide:low] = slots(beside + 1)
    held[0:part, low:tail] = slots((chip ^ 6) + core)
    own_asks[...] = slots(chip + core)


def context_pieces(packs, part, context_rows, low, tail):
    rest = part - context_rows
    first = (
        (0, context_rows, 0, packs.at[0:context_rows, tail:]),
        (0, context_rows, LANES, packs.at[part : part + context_rows, tail:]),
        (0, rest, 2 * LANES, packs.at[context_rows:part, tail:]),
        (rest, rest, 2 * LANES, packs.at[part + context_rows :, tail:]),
    )
    return first, ((0, context_rows, 0, packs.at[part : part + context_rows, low:tail]),)


def bundle_kernel(width, context_rows, first, after, out, forward):
    core = lax.axis_index("slab") % 2
    part = forward.shape[0]
    rest = part - context_rows
    total = first.shape[1]
    low, tail = total - LANES - width, total - LANES
    wide = low - width
    forward[:, 0:wide] = first[pl.ds(pl.multiple_of(core * part, part), part), 0:wide]
    forward[:, wide:low] = first[0:part, low:tail]
    out[...] = first[...]
    pieces = context_pieces(first, part, context_rows, low, tail)

    @pl.when(core == 0)
    def _():
        left, middle, upper, lower = (piece[3] for piece in pieces[0])
        forward[0:context_rows, low : low + LANES] = left[...]
        forward[0:context_rows, low + LANES :] = middle[...]
        forward[context_rows:, low : low + LANES] = upper[...]
        forward[context_rows:, low + LANES :] = lower[...]

    @pl.when(core == 1)
    def _():
        whole = pieces[1][0][3]
        forward[0:context_rows, low:] = whole[:, 0 : 2 * LANES]
        forward[context_rows:, low : low + LANES] = whole[0:rest, 2 * LANES :]
        forward[context_rows:, low + LANES :] = whole[rest:, 2 * LANES :]


def split_kernel(piece, after, left, right):
    left[...] = piece[:, 0 : left.shape[1]]
    right[...] = piece[:, left.shape[1] :]


def teacher_kernel(
    capacity, head_size, tokens, masked, slot_keys, block0, message, block2, block3,
    own_core, peer_core, queries, keys, values, attended,
):
    cam, slab = position()
    wide, base = keys.shape[1], message.shape[0] - tokens
    pieces = [message.at[base:, number * wide : (number + 1) * wide] for number in range(3)]
    for relation, block in enumerate((block0, None, block2, block3)):
        if relation == 1:
            key_part, value_part, query_part = pieces
            query_part = query_part.at[0:masked]
        else:
            key_part, value_part = block.at[0:tokens], block.at[tokens : 2 * tokens]
            query_part = block.at[2 * tokens : 2 * tokens + masked]
        keys[relation * tokens : (relation + 1) * tokens] = key_part[...]
        values[relation * tokens : (relation + 1) * tokens] = value_part[...]
        start = pl.multiple_of((slab ^ relation) * masked, masked)
        queries[pl.ds(start, masked)] = query_part[...]
    scale = math.log2(math.e) / math.sqrt(head_size)
    chunk = 2 * masked
    for half in range(2):
        rows = slice(half * chunk, (half + 1) * chunk)
        total = [jnp.zeros((chunk, LANES), jnp.float32) for _ in range(attended.shape[1] // LANES)]
        for low, high, start, stop in head_windows(4, head_size):
            window = inside((chunk, stop - start), start, low, high)
            picked = jnp.where(window, queries[rows, start:stop].astype(jnp.float32), 0.0)
            scores = rows_dot(picked.astype(jnp.bfloat16), keys[:, start:stop])
            terms, weight = softmax_terms(scores, scale)
            mixed = dot(terms, values[:, start:stop]) / weight
            mixed = jnp.where(window, mixed, 0.0)
            for tile in range(start // LANES, stop // LANES):
                total[tile] += mixed[:, tile * LANES - start : (tile + 1) * LANES - start]
        attended[rows] = jnp.concatenate(total, axis=1).astype(jnp.bfloat16)
    for flip, out in enumerate((own_core, peer_core)):
        for relation in range(4):
            owner = (cam * 4 + slab) ^ (relation * 2 + flip)
            for half in range(2):
                picker = slot_picker(slot_keys[pl.ds(2 * cam + half, 1), :], owner, capacity, 8 * capacity)
                at = (relation * 2 + half) * 2 * capacity
                out[at : at + 2 * capacity] = dot(
                    picker, attended[half * chunk : (half + 1) * chunk]
                ).astype(jnp.bfloat16)


def pass_kernel(rows, after, out):
    out[...] = rows[...]


def project_kernel(
    capacity, slot_keys, own_slots, peer_slots, w_own, w_cam, w_core, w_both, resid_own,
    out0, out1, out2, out3, weight, resid_pair, total,
):
    cam, slab = position()
    core, chip = slab % 2, slab // 2
    width = w_own.shape[1]
    part = width // 8
    half = own_slots.shape[1]
    for base, same, crossed in ((0, w_own, w_cam), (half, w_core, w_both)):
        weight[pl.ds(pl.multiple_of(base + cam * part, 16), part)] = same[0:part]
        weight[pl.ds(pl.multiple_of(base + (1 - cam) * part, 16), part)] = crossed[0:part]
        weight[base + 2 * part : base + half] = jnp.zeros((half - 2 * part, width), jnp.bfloat16)
    rows = resid_own.shape[0]
    resid_pair[pl.ds(pl.multiple_of(core * rows, rows), rows)] = resid_own[...]
    resid_pair[pl.ds(pl.multiple_of((1 - core) * rows, rows), rows)] = w_core[
        w_own.shape[0] : w_own.shape[0] + rows
    ]
    key_row = slot_keys[pl.ds(2 * cam + chip, 1), :]
    block = out0.shape[0]
    for relation, out in ((3, out3), (2, out2), (1, out1), (0, out0)):
        at = relation * block
        total[...] = dot(own_slots[at : at + block], weight[0:half]) + dot(
            peer_slots[at : at + block], weight[half:]
        )
        owner = (cam * 4 + slab) ^ (relation * 2)
        picker = slot_picker(key_row, owner, capacity, 8 * capacity)
        own_rows = pl.ds(pl.multiple_of(chip * 2 * capacity, 8), 2 * capacity)
        total[own_rows] = total[own_rows] + dot(picker, resid_pair[...])
        out[...] = total[...].astype(jnp.bfloat16)


def predict_kernel(
    base, context_rows, message, own_pack, own_asks, first, third, peer_left, peer_right, peers, out,
    queries, weights, context, peer_pack, peer_third,
):
    cam, slab = position()
    core = slab % 2
    own = cam * 4 + slab
    chip = own - core
    part, wide = third.shape[0], weights.shape[1]
    width = context.shape[1]
    rest = part - context_rows
    low, tail = wide + width, wide + 2 * width

    def place(source, packs, at):
        weights[pl.ds(pl.multiple_of(source * part, part), part)] = packs[:, 0:wide]
        start = pl.multiple_of(source * context_rows, context_rows)
        context[pl.ds(start, context_rows), 0 : 2 * LANES] = packs[0:context_rows, at:]
        for number in range(2):
            lanes = slice(at + number * LANES, at + (number + 1) * LANES)
            rows = pl.ds(pl.multiple_of(start + number * rest, rest), rest)
            context[rows, 2 * LANES :] = packs[context_rows:, lanes]

    def place_pair(source, packs):
        for flip, pieces in enumerate(context_pieces(packs, part, context_rows, low, tail)):
            rows = pl.ds(pl.multiple_of((source + flip) * part, part), part)
            weights[rows] = packs[flip * part : (flip + 1) * part, 0:wide]
            start = pl.multiple_of((source + flip) * context_rows, context_rows)
            for skip, count, lane, piece in pieces:
                rows = pl.ds(pl.multiple_of(start + skip, rest), count)
                context[rows, lane : lane + piece.shape[1]] = piece[...]

    def place_asks(source, asked):
        queries[pl.ds(pl.multiple_of(source // 2 * part, part), part)] = asked

    for number, start in enumerate(range(0, own_pack.shape[1], message.shape[1])):
        stop = min(start + message.shape[1], own_pack.shape[1])
        at = base + number * part
        peer_pack[:, start:stop] = message[at : at + part, 0 : stop - start]
    peer_third[:, 0 : peer_left.shape[1]] = peer_left[...]
    peer_third[:, peer_left.shape[1] :] = peer_right[...]
    place(own, own_pack, tail)
    place(own ^ 1, peer_pack, tail)
    place(own ^ 6, third, low)
    place(own ^ 7, peer_third, low)
    along, across = jnp.where(core == 0, 2, 4), jnp.where(core == 0, 4, 2)
    place_pair(chip ^ along, first)
    place_pair(chip ^ across, peers)
    mine = pl.ds(pl.multiple_of(core * part, part), part)
    place_asks(chip, own_asks[...])
    place_asks(chip ^ 6, third[:, wide:low])
    place_asks(chip ^ along, first[mine, wide:low])
    place_asks(chip ^ across, peers[mine, wide:low])
    head_size = width // P_HEADS
    scale = math.log2(math.e) / math.sqrt(head_size)
    asked = dot(queries[...], weights[:, 0:width]).astype(jnp.bfloat16)
    seen_keys = dot(context[...], weights[:, width : 2 * width]).astype(jnp.bfloat16)
    seen_values = dot(context[...], weights[:, 2 * width : 3 * width]).astype(jnp.bfloat16)
    total = [jnp.zeros((asked.shape[0], LANES), jnp.float32) for _ in range(width // LANES)]
    for low, high, start, stop in head_windows(P_HEADS, head_size):
        window = inside((asked.shape[0], stop - start), start, low, high)
        picked = jnp.where(window, asked[:, start:stop].astype(jnp.float32), 0.0)
        scores = rows_dot(picked.astype(jnp.bfloat16), seen_keys[:, start:stop])
        terms, weight = softmax_terms(scores, scale)
        mixed = dot(terms, seen_values[:, start:stop]) / weight
        total[start // LANES] += jnp.where(window, mixed, 0.0)
    attended = jnp.concatenate(total, axis=1).astype(jnp.bfloat16)
    hidden = queries[...].astype(jnp.float32) + dot(attended, weights[:, 3 * width : 4 * width])
    predicted = norm_rows(hidden).astype(jnp.bfloat16)
    out[...] = dot(predicted, weights[:, 4 * width :])


def error_rows(capacity, masked, owner, listed, predicted, near, far):
    rows = near.shape[0]
    summed = near[...].astype(jnp.float32) + far[...].astype(jnp.float32)
    shape = (rows, listed.shape[1])
    row = lax.broadcasted_iota(jnp.int32, shape, 0)
    lane = lax.broadcasted_iota(jnp.int32, shape, 1)
    same = jnp.zeros(shape, jnp.bool_)
    for group in range(4):
        same = same | (
            (row >= group * capacity)
            & (row < (group + 1) * capacity)
            & (lane >= group * masked)
            & (lane < (group + 1) * masked)
        )
    count = jnp.sum(jnp.where(same & (listed == owner), 1.0, 0.0), axis=1, keepdims=True)
    order = lax.broadcasted_iota(jnp.int32, (rows, 1), 0)
    order = order - sum(
        jnp.where(order >= group * capacity, capacity, 0) for group in range(1, 4)
    )
    filled = order.astype(jnp.float32) < count
    goal = norm_rows(summed).astype(jnp.bfloat16).astype(jnp.float32)
    return jnp.where(filled, predicted - goal, 0.0).astype(jnp.bfloat16)


def own_camera_kernel(capacity, masked, owners, predicted, near, far, out):
    cam, slab = position()
    rows = near.shape[0]
    at = pl.ds(pl.multiple_of(cam * rows, rows), rows)
    listed = owners[pl.ds(cam, 1), :]
    out[...] = error_rows(capacity, masked, cam * 4 + slab, listed, predicted[at], near, far)


def other_camera_kernel(
    capacity, masked, owners, predicted, first_rows, near, far, out, here, done
):
    cam, slab = position()
    rows = near.shape[0]
    own = pl.ds(pl.multiple_of(cam * rows, rows), rows)
    at = pl.ds(pl.multiple_of((1 - cam) * rows, rows), rows)
    early = pltpu.make_async_copy(first_rows, out.at[own], done.at[0])
    early.start()
    listed = owners[pl.ds(1 - cam, 1), :]
    here[...] = error_rows(capacity, masked, cam * 4 + slab, listed, predicted[at], near, far)
    late = pltpu.make_async_copy(here, out.at[at], done.at[1])
    late.start()
    early.wait()
    late.wait()


def call(kernel, outs, scratch, *args, far=0, copies=0, after=0, out_space=pltpu.VMEM):
    shapes = tuple(jax.ShapeDtypeStruct(shape, dtype) for shape, dtype in outs)
    near = pl.BlockSpec(memory_space=pltpu.VMEM)
    scratch_shapes = [pltpu.VMEM(shape, dtype) for shape, dtype in scratch]
    if copies:
        scratch_shapes.append(pltpu.SemaphoreType.DMA((copies,)))
    if far:
        args = [pltpu.with_memory_space_constraint(arg, pltpu.HBM) for arg in args[:far]] + list(args[far:])
    return pl.pallas_call(
        kernel,
        out_shape=shapes,
        in_specs=[pl.BlockSpec(memory_space=pltpu.HBM)] * far
        + [near] * (len(args) - far - after)
        + [pl.BlockSpec(memory_space=pl.ANY)] * after,
        out_specs=tuple(pl.BlockSpec(memory_space=out_space) for _ in outs),
        scratch_shapes=scratch_shapes,
        compiler_params=pltpu.CompilerParams(vmem_limit_bytes=40 * 2**20),
    )(*args)


def send(rows, flip):
    return lax.ppermute(rows, ("cam", "slab"), [(source, source ^ flip) for source in range(8)])


def send_by_core(rows, even, odd):
    pairs = [(source, source ^ (odd if source % 2 else even)) for source in range(8)]
    return lax.ppermute(rows, ("cam", "slab"), pairs)


def paired_shards(
    t_query, t_key, t_value, t_resid, w_out_teacher, pred_query, pred_context,
    w_query, w_key, w_value, w_out, w_proj, mask_list, owners,
):
    bf16, f32 = jnp.bfloat16, jnp.float32
    tokens, width = t_key.shape[1:]
    masked, pred_width = pred_query.shape[1:]
    capacity = masked // 4
    quarter = width // 8
    head_size = width // HEADS
    context_rows = pred_context.shape[1]
    padded = -(-2 * quarter // LANES) * LANES
    block_rows = 2 * tokens + masked
    block = ((block_rows, padded), bf16)
    weight_rows = w_query.shape[0]
    weight_width = 4 * pred_width + w_proj.shape[1]
    pack_width = weight_width + 2 * pred_width + context_rows * pred_width // weight_rows
    pack_at = quarter + masked
    message_rows = pack_at - pack_width // -width * weight_rows + tokens
    shard = ((weight_rows, pack_width), bf16)
    block0, block2, block3, resid_rows, slot_keys, pack, message, w_here = call(
        functools.partial(pack_kernel, capacity),
        [
            block, block, block, ((masked, width), bf16), ((4, 2 * masked), jnp.int32), shard,
            ((message_rows, width), bf16), ((quarter, width), bf16),
        ],
        [
            ((block_rows, width), bf16), ((4, block_rows, padded), bf16), ((tokens, width), bf16),
            ((tokens, width), bf16), (mask_list.shape, jnp.int32), (owners.shape, jnp.int32),
        ],
        t_query[0], t_key[0], t_value[0], t_resid[0], mask_list, owners,
        w_query, w_key, w_value, w_out, w_proj, pred_query[0], pred_context[0], w_out_teacher,
        far=14, copies=18,
    )
    other2, other3 = send(block2, 2), send(block3, 3)
    w_cam = send(w_here, 4)
    peer_message = send(message, 1)
    pair = ((2 * weight_rows, weight_width + 2 * pred_width + LANES), bf16)
    forwarded = ((weight_rows, weight_width + pred_width + 2 * LANES), bf16)
    asked = ((2 * capacity, pred_width), bf16)
    held, own_asks = call(
        functools.partial(hold_kernel, capacity, pack_at, pred_width, context_rows),
        [pair, asked],
        [shard, ((2 * masked, pred_width), bf16)],
        slot_keys, pack, peer_message, other2,
        after=1,
    )
    first = send_by_core(held, 2, 4)
    slots = ((16 * capacity, padded), bf16)
    own_slots, away_slots = call(
        functools.partial(teacher_kernel, capacity, head_size, tokens, masked),
        [slots, slots],
        [
            ((4 * masked, padded), bf16), ((4 * tokens, padded), bf16), ((4 * tokens, padded), bf16),
            ((4 * masked, padded), bf16),
        ],
        slot_keys, block0, peer_message, other2, other3,
    )
    peer_slots = send(away_slots, 1)
    (w_pass,) = call(pass_kernel, [((quarter, width), bf16)], [], w_cam, own_slots, after=1)
    w_both = send(w_pass, 1)
    part = ((4 * capacity, width), bf16)
    part0, part1, part2, part3 = call(
        functools.partial(project_kernel, capacity),
        [part] * 4,
        [((2 * padded, width), bf16), ((2 * masked, width), bf16), ((4 * capacity, width), f32)],
        slot_keys, own_slots, peer_slots, w_here, w_cam, peer_message,
        w_both, resid_rows,
    )
    far1, far2, far3 = send(part1, 2), send(part2, 4), send(part3, 6)
    bundle, forward = call(
        functools.partial(bundle_kernel, pred_width, context_rows),
        [pair, forwarded], [], first, part0,
        after=1,
    )
    peers, third = send(bundle, 1), send_by_core(forward, 4, 2)
    whole = forwarded[0][1]
    left_width = whole // 2 // LANES * LANES
    halves = [((weight_rows, lanes), bf16) for lanes in (left_width, whole - left_width)]
    left, right = call(
        split_kernel, halves, [], third, peers, after=1
    )
    (predicted,) = call(
        functools.partial(predict_kernel, pack_at, context_rows),
        [((8 * capacity, width), f32)],
        [
            ((8 * capacity, pred_width), bf16), ((8 * weight_rows, weight_width), bf16),
            ((8 * context_rows, pred_width), bf16), shard, forwarded,
        ],
        peer_message, pack, own_asks, first, third, send(left, 1), send(right, 1), peers,
    )
    (first_rows,) = call(
        functools.partial(own_camera_kernel, capacity, masked),
        [part],
        [],
        owners, predicted, part0, far1,
    )
    (errors,) = call(
        functools.partial(other_camera_kernel, capacity, masked),
        [((8 * capacity, width), bf16)],
        [part],
        owners, predicted, first_rows, far3, far2,
        copies=2, out_space=pltpu.HBM,
    )
    return errors[None, None]


def solution(mesh):
    placed = (
        P(("clip", "cam"), "slab", None),
        P(("clip", "cam"), "slab", None),
        P(("clip", "cam"), "slab", None),
        P(("clip", "cam"), "slab", None),
        P(("cam", "slab"), None),
        P(("clip", "cam"), "slab", None),
        P(("clip", "cam"), "slab", None),
        P(("cam", "slab"), None),
        P(("cam", "slab"), None),
        P(("cam", "slab"), None),
        P(("cam", "slab"), None),
        P(("cam", "slab"), None),
        P(("clip", "cam"), "slab"),
        P("clip", None),
    )
    small = (mesh.shape["cam"], mesh.shape["slab"]) == (2, 4) and mesh.shape["clip"] % 2 == 0
    return jax.shard_map(
        paired_shards if small else shards,
        mesh=mesh,
        in_specs=placed,
        out_specs=P(("clip", "cam"), "slab", None, None),
        check_vma=False,
    )
```

```python
import functools
import math

import jax
import jax.numpy as jnp
from jax import lax
from jax.experimental import pallas as pl
from jax.experimental.pallas import tpu as pltpu
from jax.sharding import PartitionSpec as P

HEADS = 16
P_HEADS = 12
LANES = 128
FOLD = 16


def norm_rows(values_in):
    average = jnp.mean(values_in, axis=-1, keepdims=True)
    centered = values_in - average
    variance = jnp.mean(centered * centered, axis=-1, keepdims=True)
    return centered * lax.rsqrt(variance + 1e-06)


def empty_state(row_count, head_count, head_size):
    return (
        jnp.full((row_count, head_count), -1e30, jnp.float32),
        jnp.zeros((row_count, head_count), jnp.float32),
        jnp.zeros((row_count, head_count, head_size), jnp.float32),
    )


def attend_block(state_now, query_heads, key_rows, value_rows):
    head_count = query_heads.shape[1]
    head_size = query_heads.shape[2]
    running_max, weight_sum, accumulated = state_now
    for offset in range(0, key_rows.shape[0], 512):
        key_block = key_rows[offset : offset + 512].reshape(-1, head_count, head_size)
        value_block = value_rows[offset : offset + 512].reshape(-1, head_count, head_size)
        scores = jnp.einsum(
            "rhd,khd->rhk", query_heads, key_block, preferred_element_type=jnp.float32
        ) / math.sqrt(head_size)
        new_max = jnp.maximum(running_max, jnp.max(scores, axis=2))
        rescale = jnp.exp(running_max - new_max)
        exponent = jnp.exp(scores - new_max[:, :, None])
        weight_sum = weight_sum * rescale + jnp.sum(exponent, axis=2)
        accumulated = accumulated * rescale[:, :, None] + jnp.einsum(
            "rhk,khd->rhd",
            exponent.astype(jnp.bfloat16),
            value_block,
            preferred_element_type=jnp.float32,
        )
        running_max = new_max
    return (running_max, weight_sum, accumulated)


def finish_heads(weight_sum, accumulated):
    mixed = accumulated / weight_sum[:, :, None]
    return mixed.reshape(mixed.shape[0], -1).astype(jnp.bfloat16)


def shards(
    t_query,
    t_key,
    t_value,
    t_resid,
    w_out_teacher,
    pred_query,
    pred_context,
    w_query,
    w_key,
    w_value,
    w_out,
    w_proj,
    mask_list,
    owners,
):
    model_width = t_query.shape[2]
    head_size = model_width // HEADS
    local_rows = mask_list[0]
    masked_count = local_rows.shape[0]
    masked_query = jnp.take(t_query[0], local_rows, axis=0)
    masked_resid = jnp.take(t_resid[0], local_rows, axis=0)
    query_heads = masked_query.reshape(masked_count, HEADS, head_size)
    pieces = (
        lax.all_gather(t_key[0], "slab", axis=0, tiled=True),
        lax.all_gather(t_value[0], "slab", axis=0, tiled=True),
    )
    running_max, weight_sum, accumulated = attend_block(
        empty_state(masked_count, HEADS, head_size), query_heads, pieces[0], pieces[1]
    )
    teacher_attended = finish_heads(weight_sum, accumulated)
    projected = jnp.dot(
        teacher_attended,
        lax.all_gather(w_out_teacher, ("cam", "slab"), axis=0, tiled=True),
        preferred_element_type=jnp.float32,
    )
    targets = norm_rows(masked_resid.astype(jnp.float32) + projected).astype(jnp.bfloat16)
    devices = lax.axis_size(("cam", "slab"))
    capacity = 2 * masked_count // devices
    myself = lax.axis_index(("cam", "slab"))
    own_dest = lax.dynamic_index_in_dim(
        owners.reshape(devices, masked_count), myself, 0, keepdims=False
    )
    earlier = jnp.tril(jnp.ones((masked_count, masked_count), jnp.bool_), -1)
    same_owner = own_dest[:, None] == own_dest[None, :]
    order_rank = jnp.sum((same_owner & earlier).astype(jnp.int32), axis=1)
    slot_index = own_dest * capacity + order_rank
    slot_total = devices * capacity
    query_rows = pred_query[0]
    pred_width = query_rows.shape[1]
    full_query, full_key, full_value, full_out, full_proj = (
        lax.all_gather(w_query, ("cam", "slab"), axis=0, tiled=True),
        lax.all_gather(w_key, ("cam", "slab"), axis=0, tiled=True),
        lax.all_gather(w_value, ("cam", "slab"), axis=0, tiled=True),
        lax.all_gather(w_out, ("cam", "slab"), axis=0, tiled=True),
        lax.all_gather(w_proj, ("cam", "slab"), axis=0, tiled=True),
    )
    pred_head = pred_width // P_HEADS
    pred_heads = (
        jnp.dot(query_rows, full_query, preferred_element_type=jnp.float32)
        .astype(jnp.bfloat16)
        .reshape(masked_count, P_HEADS, pred_head)
    )
    start_state = empty_state(masked_count, P_HEADS, pred_head)
    context = lax.all_gather(pred_context[0], ("cam", "slab"), axis=0, tiled=True)
    context_keys = jnp.dot(context, full_key, preferred_element_type=jnp.float32)
    context_values = jnp.dot(context, full_value, preferred_element_type=jnp.float32)
    running_max, weight_sum, accumulated = attend_block(
        start_state,
        pred_heads,
        context_keys.astype(jnp.bfloat16),
        context_values.astype(jnp.bfloat16),
    )
    pred_attended = finish_heads(weight_sum, accumulated)
    pred_hidden = query_rows.astype(jnp.float32) + jnp.dot(
        pred_attended, full_out, preferred_element_type=jnp.float32
    )
    predicted = norm_rows(pred_hidden).astype(jnp.bfloat16)
    difference = jnp.dot(
        predicted, full_proj, preferred_element_type=jnp.float32
    ) - targets.astype(jnp.float32)
    sent = (
        jnp.zeros((slot_total, model_width), jnp.bfloat16)
        .at[slot_index]
        .set(difference.astype(jnp.bfloat16))
        .reshape(devices, capacity, model_width)
    )
    errors = lax.all_to_all(sent, ("cam", "slab"), split_axis=0, concat_axis=0, tiled=True)
    return errors.reshape(1, 1, slot_total, model_width)


def rows_dot(left, right):
    return lax.dot_general(
        left, right, (((1,), (1,)), ((), ())), preferred_element_type=jnp.float32
    )


def dot(left, right):
    return jnp.dot(left, right, preferred_element_type=jnp.float32)


def position():
    return lax.axis_index("cam"), lax.axis_index("slab")


def head_windows(head_count, head_size):
    windows = []
    for head in range(head_count):
        low, high = head * head_size, (head + 1) * head_size
        start = low // LANES * LANES
        windows.append((low, high, start, -(-high // LANES) * LANES))
    return windows


def inside(shape, start, low, high):
    lane = lax.broadcasted_iota(jnp.int32, shape, 1) + start
    return (lane >= low) & (lane < high)


def softmax_terms(scores, scale):
    peak = jnp.max(scores, axis=1, keepdims=True)
    terms = jnp.exp2((scores - peak) * scale)
    return terms.astype(jnp.bfloat16), jnp.sum(terms, axis=1, keepdims=True)


def slot_picker(key_row, owner, capacity, slot_total):
    shape = (2 * capacity, key_row.shape[1])
    row = lax.broadcasted_iota(jnp.int32, shape, 0)
    late = row >= capacity
    wanted = owner * capacity + row + jnp.where(late, slot_total - capacity, 0)
    return jnp.where(key_row == wanted, 1.0, 0.0).astype(jnp.bfloat16)


def pack_kernel(
    capacity, query, key, value, resid, mask, owners, wq, wk, wv, wo, wp, asks, context, w_far,
    block0, block2, block3, resid_rows, slot_keys, pack, message, w_here,
    stack, blocks, query_here, resid_here, mask_here, owners_here, done,
):
    cam, slab = position()
    tokens, width = key.shape
    masked, pred_width = asks.shape
    quarter = width // 8
    context_rows = context.shape[0]
    row_total = stack.shape[0]
    half = masked // 2
    moves = [
        (mask, mask_here),
        (owners, owners_here),
        (query, query_here),
        (key, stack.at[0:tokens]),
        (value, stack.at[tokens : 2 * tokens]),
        (resid, resid_here),
        (w_far, w_here),
        (w_far, message.at[0:quarter]),
    ]
    at = 0
    for part in (wq, wk, wv, wo, wp):
        moves.append((part, pack.at[:, at : at + part.shape[1]]))
        at += part.shape[1]
    moves.append((asks.at[0:half], pack.at[:, at : at + pred_width]))
    moves.append((asks.at[half:], pack.at[:, at + pred_width : at + 2 * pred_width]))
    at += 2 * pred_width
    split, rest = pack.shape[1] - at, half - context_rows
    moves.append((context.at[:, 0:split], pack.at[0:context_rows, at:]))
    for number in range(context_rows // rest):
        lanes = slice(at + number * (pred_width - split), at + (number + 1) * (pred_width - split))
        moves.append(
            (
                context.at[number * rest : (number + 1) * rest, split:],
                pack.at[context_rows:, lanes],
            )
        )
    copies = [
        pltpu.make_async_copy(source, target, done.at[number])
        for number, (source, target) in enumerate(moves)
    ]
    for copy in copies:
        copy.start()
    token = lax.broadcasted_iota(jnp.int32, (tokens, masked), 0)
    copies[0].wait()
    chosen = jnp.where(token == mask_here[...], 1.0, 0.0).T.astype(jnp.bfloat16)
    copies[1].wait()
    listed = owners.shape[1]
    before = lax.broadcasted_iota(jnp.int32, (listed, listed), 0)
    after = lax.broadcasted_iota(jnp.int32, (listed, listed), 1)
    group = sum((before >= edge).astype(jnp.int32) for edge in range(masked, listed, masked))
    group_after = sum((after >= edge).astype(jnp.int32) for edge in range(masked, listed, masked))
    precedes = jnp.where((before < after) & (group == group_after), 1.0, 0.0)
    precedes = precedes.astype(jnp.bfloat16)
    lane = lax.broadcasted_iota(jnp.int32, (1, listed), 1)
    odd = ((lane >= masked) & (lane < 2 * masked)) | (lane >= 3 * masked)
    device = lax.broadcasted_iota(jnp.int32, (8, listed), 0)
    for camera in range(2):
        owner_row = owners_here[camera : camera + 1, :]
        owned = jnp.where(device == owner_row, 1.0, 0.0)
        counted = dot(owned.astype(jnp.bfloat16), precedes)
        rank = jnp.sum(owned * counted, axis=0, keepdims=True).astype(jnp.int32)
        keys = owner_row * capacity + rank + jnp.where(odd, 8 * capacity, 0)
        slot_keys[2 * camera : 2 * camera + 1, :] = keys[:, 0 : 2 * masked]
        slot_keys[2 * camera + 1 : 2 * camera + 2, :] = keys[:, 2 * masked :]
    for copy in copies[2:5]:
        copy.wait()
    stack[2 * tokens :] = dot(chosen, query_here[...]).astype(jnp.bfloat16)
    pad = blocks.shape[2] - 2 * quarter
    for other in range(4):
        first = stack[:, other * quarter : (other + 1) * quarter]
        second = stack[:, (other + 4) * quarter : (other + 5) * quarter]
        whole = jnp.concatenate(
            [first, second, jnp.zeros((row_total, pad), jnp.bfloat16)], axis=1
        )
        blocks[other] = whole
        for number in range(2 * quarter // pad):
            rows = slice(number * FOLD, (number + 1) * FOLD)
            blocks[other, rows, 2 * quarter :] = whole[
                row_total - FOLD :, number * pad : (number + 1) * pad
            ]
    for relation, out in ((0, block0), (2, block2), (3, block3)):
        out[...] = blocks[slab ^ relation, 0 : out.shape[0]]
    core_block = blocks.at[slab ^ 1]
    for copy in copies[5:]:
        copy.wait()
    picked = dot(chosen, resid_here[...]).astype(jnp.bfloat16)
    resid_rows[...] = picked
    base = quarter + masked
    message[quarter:base] = picked
    count, total = pack.shape
    for low in range(0, total, width):
        high = min(low + width, total)
        message[base : base + count, 0 : high - low] = pack[:, low:high]
        if high - low < width:
            message[base : base + count, high - low :] = jnp.zeros(
                (count, width - high + low), jnp.bfloat16
            )
        base += count
    wide = core_block.shape[1]
    for number in range(3):
        low, high = number * tokens, min((number + 1) * tokens, row_total)
        lanes = slice(number * wide, (number + 1) * wide)
        message[base : base + high - low, lanes] = core_block[low:high]
    message[base + masked :, 2 * wide : 3 * wide] = jnp.zeros((tokens - masked, wide), jnp.bfloat16)
    message[base:, 3 * wide :] = jnp.zeros((tokens, width - 3 * wide), jnp.bfloat16)


def hold_kernel(
    capacity, base, width, context_rows, slot_keys, pack, message, after, held, own_asks,
    peer, pair,
):
    cam, slab = position()
    core = slab % 2
    chip = cam * 4 + slab - core
    part, total = pack.shape
    lanes = message.shape[1]
    for number, low in enumerate(range(0, total, lanes)):
        high = min(low + lanes, total)
        at = base + number * part
        peer[:, low:high] = message[at : at + part, 0 : high - low]
    wide = total - 2 * width - context_rows * width // part
    low, tail = wide + width, wide + 2 * width
    rest = part - context_rows

    def fill(source, packs):
        held[pl.ds(pl.multiple_of(source * part, part), part), 0:wide] = packs[:, 0:wide]
        for number in range(2):
            start = pl.multiple_of((2 * source + number) * part, part)
            pair[pl.ds(start, part)] = packs[:, wide + number * width : wide + (number + 1) * width]

    fill(core, pack)
    fill(1 - core, peer)
    held[part:, low:] = jnp.zeros((part, held.shape[1] - low), jnp.bfloat16)

    def contexts(first, second):
        split = 2 * LANES
        held[0:context_rows, tail:] = first[0:context_rows, tail : tail + LANES]
        held[part : part + context_rows, tail:] = first[0:context_rows, tail + LANES :]
        held[context_rows:part, tail:] = first[context_rows:, tail : tail + LANES]
        held[part + context_rows :, tail:] = first[context_rows:, tail + LANES :]
        held[part : part + context_rows, low : low + split] = second[0:context_rows, tail:]
        for number in range(2):
            at = part + number * rest
            source = slice(tail + number * LANES, tail + (number + 1) * LANES)
            held[at : at + rest, low + split : tail] = second[context_rows:, source]

    @pl.when(core == 0)
    def _():
        contexts(pack, peer)

    @pl.when(core == 1)
    def _():
        contexts(peer, pack)

    key_row = slot_keys[pl.ds(2 * cam + slab // 2, 1), :]

    def slots(owner):
        picker = slot_picker(key_row, owner, capacity, 8 * capacity)
        return dot(picker, pair[...]).astype(jnp.bfloat16)

    beside = chip ^ jnp.where(core == 0, 2, 4)
    held[0:part, wide:low] = slots(beside)
    held[part:, wide:low] = slots(beside + 1)
    held[0:part, low:tail] = slots((chip ^ 6) + core)
    own_asks[...] = slots(chip + core)


def context_pieces(packs, part, context_rows, low, tail):
    rest = part - context_rows
    first = (
        (0, context_rows, 0, packs.at[0:context_rows, tail:]),
        (0, context_rows, LANES, packs.at[part : part + context_rows, tail:]),
        (0, rest, 2 * LANES, packs.at[context_rows:part, tail:]),
        (rest, rest, 2 * LANES, packs.at[part + context_rows :, tail:]),
    )
    return first, ((0, context_rows, 0, packs.at[part : part + context_rows, low:tail]),)


def bundle_kernel(width, context_rows, first, after, out, forward):
    core = lax.axis_index("slab") % 2
    part = forward.shape[0]
    rest = part - context_rows
    total = first.shape[1]
    low, tail = total - LANES - width, total - LANES
    wide = low - width
    forward[:, 0:wide] = first[pl.ds(pl.multiple_of(core * part, part), part), 0:wide]
    forward[:, wide:low] = first[0:part, low:tail]
    out[...] = first[...]
    pieces = context_pieces(first, part, context_rows, low, tail)

    @pl.when(core == 0)
    def _():
        left, middle, upper, lower = (piece[3] for piece in pieces[0])
        forward[0:context_rows, low : low + LANES] = left[...]
        forward[0:context_rows, low + LANES :] = middle[...]
        forward[context_rows:, low : low + LANES] = upper[...]
        forward[context_rows:, low + LANES :] = lower[...]

    @pl.when(core == 1)
    def _():
        whole = pieces[1][0][3]
        forward[0:context_rows, low:] = whole[:, 0 : 2 * LANES]
        forward[context_rows:, low : low + LANES] = whole[0:rest, 2 * LANES :]
        forward[context_rows:, low + LANES :] = whole[rest:, 2 * LANES :]


def split_kernel(piece, after, left, right):
    left[...] = piece[:, 0 : left.shape[1]]
    right[...] = piece[:, left.shape[1] :]


def teacher_kernel(
    capacity, head_size, tokens, masked, slot_keys, block0, message, block2, block3,
    own_core, peer_core, queries, keys, values, attended,
):
    cam, slab = position()
    wide, base = keys.shape[1], message.shape[0] - tokens
    pieces = [message.at[base:, number * wide : (number + 1) * wide] for number in range(3)]
    for relation, block in enumerate((block0, None, block2, block3)):
        if relation == 1:
            key_part, value_part, query_part = pieces
            query_part = query_part.at[0:masked]
        else:
            key_part, value_part = block.at[0:tokens], block.at[tokens : 2 * tokens]
            query_part = block.at[2 * tokens :]
        keys[relation * tokens : (relation + 1) * tokens] = key_part[...]
        values[relation * tokens : (relation + 1) * tokens] = value_part[...]
        start = pl.multiple_of((slab ^ relation) * masked, masked)
        direct = query_part.shape[0]
        queries[pl.ds(start, direct)] = query_part[...]
        if direct < masked:
            last = pl.ds(pl.multiple_of(start + direct, FOLD), FOLD)
            used = 4 * head_size
            queries[last, used:] = jnp.zeros((FOLD, wide - used), jnp.bfloat16)
            for number in range(used // (wide - used)):
                rows = slice(number * FOLD, (number + 1) * FOLD)
                lanes = slice(number * (wide - used), (number + 1) * (wide - used))
                queries[last, lanes] = block[rows, used:]
    scale = math.log2(math.e) / math.sqrt(head_size)
    chunk = 2 * masked
    for half in range(2):
        rows = slice(half * chunk, (half + 1) * chunk)
        total = [jnp.zeros((chunk, LANES), jnp.float32) for _ in range(attended.shape[1] // LANES)]
        for low, high, start, stop in head_windows(4, head_size):
            window = inside((chunk, stop - start), start, low, high)
            picked = jnp.where(window, queries[rows, start:stop].astype(jnp.float32), 0.0)
            scores = rows_dot(picked.astype(jnp.bfloat16), keys[:, start:stop])
            terms, weight = softmax_terms(scores, scale)
            mixed = dot(terms, values[:, start:stop]) / weight
            mixed = jnp.where(window, mixed, 0.0)
            for tile in range(start // LANES, stop // LANES):
                total[tile] += mixed[:, tile * LANES - start : (tile + 1) * LANES - start]
        attended[rows] = jnp.concatenate(total, axis=1).astype(jnp.bfloat16)
    for flip, out in enumerate((own_core, peer_core)):
        for relation in range(4):
            owner = (cam * 4 + slab) ^ (relation * 2 + flip)
            for half in range(2):
                picker = slot_picker(slot_keys[pl.ds(2 * cam + half, 1), :], owner, capacity, 8 * capacity)
                at = (relation * 2 + half) * 2 * capacity
                out[at : at + 2 * capacity] = dot(
                    picker, attended[half * chunk : (half + 1) * chunk]
                ).astype(jnp.bfloat16)


def pass_kernel(rows, after, out):
    out[...] = rows[...]


def project_kernel(
    capacity, slot_keys, own_slots, peer_slots, w_own, w_cam, w_core, w_both, resid_own,
    out0, out1, out2, out3, weight, resid_pair, total,
):
    cam, slab = position()
    core, chip = slab % 2, slab // 2
    width = w_own.shape[1]
    part = width // 8
    half = own_slots.shape[1]
    for base, same, crossed in ((0, w_own, w_cam), (half, w_core, w_both)):
        weight[pl.ds(pl.multiple_of(base + cam * part, 16), part)] = same[0:part]
        weight[pl.ds(pl.multiple_of(base + (1 - cam) * part, 16), part)] = crossed[0:part]
        weight[base + 2 * part : base + half] = jnp.zeros((half - 2 * part, width), jnp.bfloat16)
    rows = resid_own.shape[0]
    resid_pair[pl.ds(pl.multiple_of(core * rows, rows), rows)] = resid_own[...]
    resid_pair[pl.ds(pl.multiple_of((1 - core) * rows, rows), rows)] = w_core[
        w_own.shape[0] : w_own.shape[0] + rows
    ]
    key_row = slot_keys[pl.ds(2 * cam + chip, 1), :]
    block = out0.shape[0]
    for relation, out in ((3, out3), (2, out2), (1, out1), (0, out0)):
        at = relation * block
        total[...] = dot(own_slots[at : at + block], weight[0:half]) + dot(
            peer_slots[at : at + block], weight[half:]
        )
        owner = (cam * 4 + slab) ^ (relation * 2)
        picker = slot_picker(key_row, owner, capacity, 8 * capacity)
        own_rows = pl.ds(pl.multiple_of(chip * 2 * capacity, 8), 2 * capacity)
        total[own_rows] = total[own_rows] + dot(picker, resid_pair[...])
        out[...] = total[...].astype(jnp.bfloat16)


def predict_kernel(
    base, context_rows, message, own_pack, own_asks, first, third, peer_left, peer_right, peers, out,
    queries, weights, context, peer_pack, peer_third,
):
    cam, slab = position()
    core = slab % 2
    own = cam * 4 + slab
    chip = own - core
    part, wide = third.shape[0], weights.shape[1]
    width = context.shape[1]
    rest = part - context_rows
    low, tail = wide + width, wide + 2 * width

    def place(source, packs, at):
        weights[pl.ds(pl.multiple_of(source * part, part), part)] = packs[:, 0:wide]
        start = pl.multiple_of(source * context_rows, context_rows)
        context[pl.ds(start, context_rows), 0 : 2 * LANES] = packs[0:context_rows, at:]
        for number in range(2):
            lanes = slice(at + number * LANES, at + (number + 1) * LANES)
            rows = pl.ds(pl.multiple_of(start + number * rest, rest), rest)
            context[rows, 2 * LANES :] = packs[context_rows:, lanes]

    def place_pair(source, packs):
        for flip, pieces in enumerate(context_pieces(packs, part, context_rows, low, tail)):
            rows = pl.ds(pl.multiple_of((source + flip) * part, part), part)
            weights[rows] = packs[flip * part : (flip + 1) * part, 0:wide]
            start = pl.multiple_of((source + flip) * context_rows, context_rows)
            for skip, count, lane, piece in pieces:
                rows = pl.ds(pl.multiple_of(start + skip, rest), count)
                context[rows, lane : lane + piece.shape[1]] = piece[...]

    def place_asks(source, asked):
        queries[pl.ds(pl.multiple_of(source // 2 * part, part), part)] = asked

    for number, start in enumerate(range(0, own_pack.shape[1], message.shape[1])):
        stop = min(start + message.shape[1], own_pack.shape[1])
        at = base + number * part
        peer_pack[:, start:stop] = message[at : at + part, 0 : stop - start]
    peer_third[:, 0 : peer_left.shape[1]] = peer_left[...]
    peer_third[:, peer_left.shape[1] :] = peer_right[...]
    place(own, own_pack, tail)
    place(own ^ 1, peer_pack, tail)
    place(own ^ 6, third, low)
    place(own ^ 7, peer_third, low)
    along, across = jnp.where(core == 0, 2, 4), jnp.where(core == 0, 4, 2)
    place_pair(chip ^ along, first)
    place_pair(chip ^ across, peers)
    mine = pl.ds(pl.multiple_of(core * part, part), part)
    place_asks(chip, own_asks[...])
    place_asks(chip ^ 6, third[:, wide:low])
    place_asks(chip ^ along, first[mine, wide:low])
    place_asks(chip ^ across, peers[mine, wide:low])
    head_size = width // P_HEADS
    scale = math.log2(math.e) / math.sqrt(head_size)
    asked = dot(queries[...], weights[:, 0:width]).astype(jnp.bfloat16)
    seen_keys = dot(context[...], weights[:, width : 2 * width]).astype(jnp.bfloat16)
    seen_values = dot(context[...], weights[:, 2 * width : 3 * width]).astype(jnp.bfloat16)
    total = [jnp.zeros((asked.shape[0], LANES), jnp.float32) for _ in range(width // LANES)]
    for low, high, start, stop in head_windows(P_HEADS, head_size):
        window = inside((asked.shape[0], stop - start), start, low, high)
        picked = jnp.where(window, asked[:, start:stop].astype(jnp.float32), 0.0)
        scores = rows_dot(picked.astype(jnp.bfloat16), seen_keys[:, start:stop])
        terms, weight = softmax_terms(scores, scale)
        mixed = dot(terms, seen_values[:, start:stop]) / weight
        total[start // LANES] += jnp.where(window, mixed, 0.0)
    attended = jnp.concatenate(total, axis=1).astype(jnp.bfloat16)
    hidden = queries[...].astype(jnp.float32) + dot(attended, weights[:, 3 * width : 4 * width])
    predicted = norm_rows(hidden).astype(jnp.bfloat16)
    out[...] = dot(predicted, weights[:, 4 * width :])


def error_rows(capacity, masked, owner, listed, predicted, near, far):
    rows = near.shape[0]
    summed = near[...].astype(jnp.float32) + far[...].astype(jnp.float32)
    shape = (rows, listed.shape[1])
    row = lax.broadcasted_iota(jnp.int32, shape, 0)
    lane = lax.broadcasted_iota(jnp.int32, shape, 1)
    same = jnp.zeros(shape, jnp.bool_)
    for group in range(4):
        same = same | (
            (row >= group * capacity)
            & (row < (group + 1) * capacity)
            & (lane >= group * masked)
            & (lane < (group + 1) * masked)
        )
    count = jnp.sum(jnp.where(same & (listed == owner), 1.0, 0.0), axis=1, keepdims=True)
    order = lax.broadcasted_iota(jnp.int32, (rows, 1), 0)
    order = order - sum(
        jnp.where(order >= group * capacity, capacity, 0) for group in range(1, 4)
    )
    filled = order.astype(jnp.float32) < count
    goal = norm_rows(summed).astype(jnp.bfloat16).astype(jnp.float32)
    return jnp.where(filled, predicted - goal, 0.0).astype(jnp.bfloat16)


def own_camera_kernel(capacity, masked, owners, predicted, near, far, out):
    cam, slab = position()
    rows = near.shape[0]
    at = pl.ds(pl.multiple_of(cam * rows, rows), rows)
    listed = owners[pl.ds(cam, 1), :]
    out[...] = error_rows(capacity, masked, cam * 4 + slab, listed, predicted[at], near, far)


def other_camera_kernel(
    capacity, masked, owners, predicted, first_rows, near, far, out, here, done
):
    cam, slab = position()
    rows = near.shape[0]
    own = pl.ds(pl.multiple_of(cam * rows, rows), rows)
    at = pl.ds(pl.multiple_of((1 - cam) * rows, rows), rows)
    early = pltpu.make_async_copy(first_rows, out.at[own], done.at[0])
    early.start()
    listed = owners[pl.ds(1 - cam, 1), :]
    here[...] = error_rows(capacity, masked, cam * 4 + slab, listed, predicted[at], near, far)
    late = pltpu.make_async_copy(here, out.at[at], done.at[1])
    late.start()
    early.wait()
    late.wait()


def call(kernel, outs, scratch, *args, far=0, copies=0, after=0, out_space=pltpu.VMEM):
    shapes = tuple(jax.ShapeDtypeStruct(shape, dtype) for shape, dtype in outs)
    near = pl.BlockSpec(memory_space=pltpu.VMEM)
    scratch_shapes = [pltpu.VMEM(shape, dtype) for shape, dtype in scratch]
    if copies:
        scratch_shapes.append(pltpu.SemaphoreType.DMA((copies,)))
    if far:
        args = [pltpu.with_memory_space_constraint(arg, pltpu.HBM) for arg in args[:far]] + list(args[far:])
    return pl.pallas_call(
        kernel,
        out_shape=shapes,
        in_specs=[pl.BlockSpec(memory_space=pltpu.HBM)] * far
        + [near] * (len(args) - far - after)
        + [pl.BlockSpec(memory_space=pl.ANY)] * after,
        out_specs=tuple(pl.BlockSpec(memory_space=out_space) for _ in outs),
        scratch_shapes=scratch_shapes,
        compiler_params=pltpu.CompilerParams(vmem_limit_bytes=40 * 2**20),
    )(*args)


def send(rows, flip):
    return lax.ppermute(rows, ("cam", "slab"), [(source, source ^ flip) for source in range(8)])


def send_by_core(rows, even, odd):
    pairs = [(source, source ^ (odd if source % 2 else even)) for source in range(8)]
    return lax.ppermute(rows, ("cam", "slab"), pairs)


def paired_shards(
    t_query, t_key, t_value, t_resid, w_out_teacher, pred_query, pred_context,
    w_query, w_key, w_value, w_out, w_proj, mask_list, owners,
):
    bf16, f32 = jnp.bfloat16, jnp.float32
    tokens, width = t_key.shape[1:]
    masked, pred_width = pred_query.shape[1:]
    capacity = masked // 4
    quarter = width // 8
    head_size = width // HEADS
    context_rows = pred_context.shape[1]
    padded = -(-2 * quarter // LANES) * LANES
    block_rows = 2 * tokens + masked
    block = ((block_rows, padded), bf16)
    folded = ((block_rows - FOLD, padded), bf16)
    weight_rows = w_query.shape[0]
    weight_width = 4 * pred_width + w_proj.shape[1]
    pack_width = weight_width + 2 * pred_width + context_rows * pred_width // weight_rows
    pack_at = quarter + masked
    message_rows = pack_at - pack_width // -width * weight_rows + tokens
    shard = ((weight_rows, pack_width), bf16)
    block0, block2, block3, resid_rows, slot_keys, pack, message, w_here = call(
        functools.partial(pack_kernel, capacity),
        [
            block, folded, folded, ((masked, width), bf16), ((4, 2 * masked), jnp.int32), shard,
            ((message_rows, width), bf16), ((quarter, width), bf16),
        ],
        [
            ((block_rows, width), bf16), ((4, block_rows, padded), bf16), ((tokens, width), bf16),
            ((tokens, width), bf16), (mask_list.shape, jnp.int32), (owners.shape, jnp.int32),
        ],
        t_query[0], t_key[0], t_value[0], t_resid[0], mask_list, owners,
        w_query, w_key, w_value, w_out, w_proj, pred_query[0], pred_context[0], w_out_teacher,
        far=14, copies=18,
    )
    other2, other3 = send(block2, 2), send(block3, 3)
    w_cam = send(w_here, 4)
    peer_message = send(message, 1)
    pair = ((2 * weight_rows, weight_width + 2 * pred_width + LANES), bf16)
    forwarded = ((weight_rows, weight_width + pred_width + 2 * LANES), bf16)
    asked = ((2 * capacity, pred_width), bf16)
    held, own_asks = call(
        functools.partial(hold_kernel, capacity, pack_at, pred_width, context_rows),
        [pair, asked],
        [shard, ((2 * masked, pred_width), bf16)],
        slot_keys, pack, peer_message, other2,
        after=1,
    )
    first = send_by_core(held, 2, 4)
    slots = ((16 * capacity, padded), bf16)
    own_slots, away_slots = call(
        functools.partial(teacher_kernel, capacity, head_size, tokens, masked),
        [slots, slots],
        [
            ((4 * masked, padded), bf16), ((4 * tokens, padded), bf16), ((4 * tokens, padded), bf16),
            ((4 * masked, padded), bf16),
        ],
        slot_keys, block0, peer_message, other2, other3,
    )
    peer_slots = send(away_slots, 1)
    (w_pass,) = call(pass_kernel, [((quarter, width), bf16)], [], w_cam, own_slots, after=1)
    w_both = send(w_pass, 1)
    part = ((4 * capacity, width), bf16)
    part0, part1, part2, part3 = call(
        functools.partial(project_kernel, capacity),
        [part] * 4,
        [((2 * padded, width), bf16), ((2 * masked, width), bf16), ((4 * capacity, width), f32)],
        slot_keys, own_slots, peer_slots, w_here, w_cam, peer_message,
        w_both, resid_rows,
    )
    far1, far2, far3 = send(part1, 2), send(part2, 4), send(part3, 6)
    bundle, forward = call(
        functools.partial(bundle_kernel, pred_width, context_rows),
        [pair, forwarded], [], first, part0,
        after=1,
    )
    peers, third = send(bundle, 1), send_by_core(forward, 4, 2)
    whole = forwarded[0][1]
    left_width = whole // 2 // LANES * LANES
    halves = [((weight_rows, lanes), bf16) for lanes in (left_width, whole - left_width)]
    left, right = call(
        split_kernel, halves, [], third, peers, after=1
    )
    (predicted,) = call(
        functools.partial(predict_kernel, pack_at, context_rows),
        [((8 * capacity, width), f32)],
        [
            ((8 * capacity, pred_width), bf16), ((8 * weight_rows, weight_width), bf16),
            ((8 * context_rows, pred_width), bf16), shard, forwarded,
        ],
        peer_message, pack, own_asks, first, third, send(left, 1), send(right, 1), peers,
    )
    (first_rows,) = call(
        functools.partial(own_camera_kernel, capacity, masked),
        [part],
        [],
        owners, predicted, part0, far1,
    )
    (errors,) = call(
        functools.partial(other_camera_kernel, capacity, masked),
        [((8 * capacity, width), bf16)],
        [part],
        owners, predicted, first_rows, far3, far2,
        copies=2, out_space=pltpu.HBM,
    )
    return errors[None, None]


def solution(mesh):
    placed = (
        P(("clip", "cam"), "slab", None),
        P(("clip", "cam"), "slab", None),
        P(("clip", "cam"), "slab", None),
        P(("clip", "cam"), "slab", None),
        P(("cam", "slab"), None),
        P(("clip", "cam"), "slab", None),
        P(("clip", "cam"), "slab", None),
        P(("cam", "slab"), None),
        P(("cam", "slab"), None),
        P(("cam", "slab"), None),
        P(("cam", "slab"), None),
        P(("cam", "slab"), None),
        P(("clip", "cam"), "slab"),
        P("clip", None),
    )
    small = (mesh.shape["cam"], mesh.shape["slab"]) == (2, 4) and mesh.shape["clip"] % 2 == 0
    return jax.shard_map(
        paired_shards if small else shards,
        mesh=mesh,
        in_specs=placed,
        out_specs=P(("clip", "cam"), "slab", None, None),
        check_vma=False,
    )
```
